32 devices in a mesh: grp: 2 (over y), ctx: 4 (over z), hd: 2 (over x), pf: 2 (over core).
Axes of the slice: x: 2, y: 2, z: 4, core: 2. Of those that a mesh axis runs over, the one named last changes fastest.
Arguments:
- latent_pages: bfloat16 [256, 16, 16, 512], P(('ctx', 'hd', 'pf'), 'grp'), parts along dimension 1, may hold values from -6 to 6
- page_target: int32 [256, 16, 1], P(None, 'grp'), parts along dimension 1, may hold values from 0 to 3; in each aligned block of 128 rows (0 to 127, 128 to 255, ..., all dimensions but the last counted through in order) at most 36 rows name the same one
- page_count: int32 [256, 16], P(None, 'grp'), parts along dimension 1, may hold values from 1 to 16
- context_length: int32 [16], P('grp'), parts along dimension 0, may hold values from 1024 to 4094
- queries: bfloat16 [2, 16, 8192], P(None, 'grp', 'hd'), parts along dimension 1, may hold values from -110 to 110
- key_up: bfloat16 [256, 1024], replicated, may hold values from -0.375 to 0.375
- value_up: bfloat16 [256, 1024], P(None, 'hd'), may hold values from -2.5 to 2.5
Outputs:
- attended: bfloat16 [2, 16, 8192], P(None, 'grp', 'hd'), parts along dimension 1
- stored_pages: bfloat16 [4608, 16, 512], P(('grp', 'ctx', 'hd', 'pf')), parts along dimension 0
The draws below stay inside these ranges and needn't reach their ends.
There are 2 independent parts, one for each index of `grp`. The reference program is written for one: setup_inputs(seed, part) draws one part's arguments, and reference() takes and returns one part's arrays. A program takes and returns all parts, laid end to end along the dimension named above; an argument that names none is the same for every part. Nothing has to cross between parts.
Inputs may be any that keep to these rules, and one draw needn't show every extreme that they name: `page_target`: among the 128 rows of one sending device (pages d*16 to (d+1)*16 - 1, every request), no value appears more than 36 times.
All inputs are finite; a program needn't handle non-finite values.
Results may differ from the reference program's by a relative error of at most 0.02.
The reference program's roundings to bfloat16 on the way count: a program that leaves them out, or rounds other values in their place, can miss the bound.
Values may be sent and summed in bfloat16 or wider, within the bound.
A program may use at most 128 MiB of HBM per device.

```python
import math
import jax
import jax.numpy as jnp
import numpy as np
from jax import lax

KVH = 8
GROUP = 8
HD_DIM = 128
LATK = 256
LATV = 256
PAGE = 16
STEPS = 2
REQS = 8
PG_DEV = 16
HEADS = 64
ROWS = 128
CAP = 36
SLOTS = 144
PPR = 256
CTXMAX = 4096
N_CTX = 4
N_HD = 2
N_PF = 2


def draw_context_length(key, part):
    key = jax.random.fold_in(key, 11)
    first_key, second_key = jax.random.split(key)
    lengths = jax.random.randint(first_key, (REQS,), CTXMAX // 4, CTXMAX - STEPS + 1)
    order = jax.random.permutation(second_key, REQS)
    slots = jnp.arange(REQS)
    lengths = jnp.where(slots == order[0], CTXMAX - STEPS, lengths)
    if REQS > 2:
        lengths = jnp.where(slots == order[1], CTXMAX // 4, lengths)
    return lengths.astype(jnp.int32)


def draw_queries(key, part):
    key = jax.random.fold_in(key, 23)
    first_key = jax.random.fold_in(key, 0)
    values = jnp.clip(jax.random.normal(first_key, (STEPS, REQS, HEADS * HD_DIM), jnp.float32), -6.0, 6.0) * 2.5
    return values.astype(jnp.bfloat16)


def place_ends(values, own_key, low, top_value):
    longest = values.shape.index(max(values.shape))
    spots = []
    for shift in (0, 1):
        where = [jax.random.randint(jax.random.fold_in(own_key, axis), (), 0, length) for axis, length in enumerate(values.shape)]
        where[longest] = (where[longest] + shift) % values.shape[longest]
        spots.append(tuple(where))
    return values.at[spots[0]].set(low).at[spots[1]].set(top_value)


def level_of(own_key, extent, shards, low, high):
    gain, own = 1.0, jax.random.fold_in(own_key, 6)
    for dim, blocks in shards:
        draws = jnp.exp(jax.random.uniform(jax.random.fold_in(own, dim), (blocks,), jnp.float32, low / len(shards), high / len(shards)))
        gain = gain * jnp.repeat(draws, extent[dim] // blocks).reshape([-1 if axis == dim else 1 for axis in range(len(extent))])
    return gain


def deal_out(own_key, own, number, rows, number_of, top, most, skew):
    sequence = jax.random.permutation(own_key, number_of)
    heavy_load, ordinary = shares(number_of, rows * top, most, skew, True), shares(number_of, rows * top, most, skew, False)
    places = jnp.arange(number_of)

    def named(sizes, offset_by):
        used = int((sizes > 0).sum())
        fixed = max(1, used // 4)
        passed = fixed + (places - fixed + offset_by * (used - fixed)) % max(1, number_of - fixed)
        return jnp.zeros((number_of,), jnp.int32).at[sequence[jnp.where(places < fixed, places, passed)]].set(jnp.asarray(sizes, jnp.int32))

    sizes = jnp.where(number % 4 == 0, named(heavy_load, number // 4), named(ordinary, number - number // 4 - 1))
    mixed = jax.random.permutation(jax.random.fold_in(own, 3), number_of)
    source_of, sink = mixed[0:number_of // 2 * 2:2], mixed[1:number_of // 2 * 2:2]
    margin = jnp.minimum(sizes[source_of] - 1, most - sizes[sink]) // 2
    margin = jnp.where((source_of == sequence[0]) | (sink == sequence[0]) | (sizes[sink] == 0), 0, jnp.maximum(margin, 0))
    passed = jax.random.randint(jax.random.fold_in(own, 4), (number_of // 2,), 0, 1 << 20) % (margin + 1)
    sizes = sizes.at[source_of].add(-passed).at[sink].add(passed)
    members = jnp.searchsorted(jnp.cumsum(sizes), jnp.arange(rows * top), side="right").astype(jnp.int32)
    grid = members.reshape(top, rows).T
    grid = grid[jax.random.permutation(jax.random.fold_in(own, 1), rows)]
    offset_by = jax.random.randint(jax.random.fold_in(own, 2), (rows, 1), 0, top)
    return jnp.take_along_axis(grid, (jnp.arange(top)[None, :] + offset_by) % top, axis=1)


def shares(count, total, bound, slope, full):
    portions = [(1 << 20) // math.isqrt(grade ** slope) + 1 for grade in range(1, count + 1)]
    largest = bound if full else min(bound, max(-(-total // count), total * portions[0] // sum(portions)))
    least = 1 if total - largest >= count - 1 else 0
    counts, surplus = [largest] + [least] * (count - 1), total - largest - least * (count - 1)
    while surplus > 0:
        free = [i for i in range(1, count) if counts[i] < largest] or [i for i in range(1, count) if counts[i] < bound]
        pool, left = sum([portions[i] for i in free]), surplus
        for i in free:
            addition = min(bound - counts[i], max(1, left * portions[i] // pool), surplus)
            counts[i] = counts[i] + addition
            surplus = surplus - addition
    return np.array(counts)


def normal_values(rng, shape, scale, reach, pieces=(), kind=jnp.bfloat16):
    drawn = scale * jax.random.normal(rng, shape, jnp.float32)
    if pieces:
        drawn = drawn * level_of(rng, shape, pieces, -0.22, 0.18)
    return jnp.clip(drawn, -reach, reach).astype(kind)


def setup_inputs(seed: int = 0, part: int = 0) -> dict:
    arg_keys = jax.random.split(jax.random.key(seed), 8)
    part_keys = jax.random.split(jax.random.fold_in(arg_keys[7], part), 8)
    latent_pages = normal_values(part_keys[0], (PPR, REQS, PAGE, LATK + LATV), 1.0, 6.0, ((0, 16),))
    page_target_keys = jax.random.split(jax.random.fold_in(part_keys[1], 1), PPR * REQS // ROWS)
    page_target_turns = jax.random.permutation(jax.random.fold_in(part_keys[1], 3), PPR * REQS // ROWS)
    page_target = jax.vmap(lambda own, number: deal_out(jax.random.fold_in(part_keys[1], 2), own, number, ROWS, N_CTX, 1, CAP, 1))(page_target_keys, page_target_turns).reshape((PPR, REQS, 1))
    page_count = place_ends(jax.random.randint(part_keys[2], (PPR, REQS), 1, PAGE + 1), jax.random.fold_in(part_keys[2], 1), 1, PAGE).astype(jnp.int32)
    context_length = draw_context_length(jax.random.fold_in(jax.random.fold_in(arg_keys[7], part), 71), part)
    queries = draw_queries(jax.random.fold_in(jax.random.fold_in(arg_keys[7], part), 71), part)
    key_up = normal_values(arg_keys[5], (LATK, KVH * HD_DIM), LATK ** -0.5, 0.375)
    value_up = normal_values(arg_keys[6], (LATV, KVH * HD_DIM), 0.25, 2.5, ((1, 2),))
    return dict(latent_pages=latent_pages, page_target=page_target, page_count=page_count, context_length=context_length, queries=queries, key_up=key_up, value_up=value_up)


def frequencies(head_width):
    exponent = jnp.arange(0, head_width, 2).astype(jnp.float32) / head_width
    inverse = jnp.power(jnp.float32(500000.0), -exponent)
    wavelength = 2.0 * math.pi / inverse
    smooth = (8192.0 / wavelength - 1.0) / 3.0
    mixed = (1.0 - smooth) * inverse / 8.0 + smooth * inverse
    return jnp.where(wavelength > 8192.0, inverse / 8.0, jnp.where(wavelength < 2048.0, inverse, mixed))

def rotate(values, position):
    halfway = values.shape[-1] // 2
    angles = position[..., None] * frequencies(values.shape[-1])
    cosine = jnp.cos(angles)
    sine_part = jnp.sin(angles)
    first_half = values[..., :halfway]
    second_half = values[..., halfway:]
    return jnp.concatenate([first_half * cosine - second_half * sine_part, second_half * cosine + first_half * sine_part], axis=-1)

def reference(latent_pages, page_target, page_count, context_length, queries, key_up, value_up):
    score_scale = 1.0 / math.sqrt(HD_DIM)
    offsets = jnp.arange(PAGE, dtype=jnp.int32)
    positions = (jnp.arange(PPR, dtype=jnp.int32)[:, None] * PAGE + offsets[None, :]).reshape(-1)
    column_count = STEPS * GROUP
    column_step = jnp.arange(column_count, dtype=jnp.int32) // GROUP
    value_heads = value_up.reshape(LATV, KVH, HD_DIM)

    def one_request(request):
        request_pages = lax.dynamic_index_in_dim(latent_pages, request, 1, keepdims=False)
        request_counts = lax.dynamic_index_in_dim(page_count, request, 1, keepdims=False)
        length = lax.dynamic_index_in_dim(context_length, request, 0, keepdims=False)
        query_rows = lax.dynamic_index_in_dim(queries, request, 1, keepdims=False)
        flat_rows = request_pages.reshape(PPR * PAGE, LATK + LATV)
        rebuilt = jnp.dot(flat_rows[:, :LATK], key_up, preferred_element_type=jnp.float32)
        rebuilt = rotate(rebuilt.reshape(-1, KVH, HD_DIM), positions.astype(jnp.float32)[:, None])
        rebuilt = lax.optimization_barrier(rebuilt.astype(jnp.bfloat16))
        valid_rows = (offsets[None, :] < request_counts[:, None]).reshape(-1)
        query_position = (length + jnp.arange(STEPS, dtype=jnp.int32)).astype(jnp.float32)
        turned = rotate(query_rows.astype(jnp.float32).reshape(STEPS, HEADS, HD_DIM), query_position[:, None])
        turned = lax.optimization_barrier(turned.astype(jnp.bfloat16))
        query_columns = turned.reshape(STEPS, KVH, GROUP, HD_DIM).transpose(1, 3, 0, 2).reshape(KVH, HD_DIM, column_count)
        scores = jnp.einsum('tkd,kdc->ktc', rebuilt.astype(jnp.float32), query_columns.astype(jnp.float32)) * score_scale
        column_limit = length + column_step
        valid_mask = valid_rows[:, None] & (positions[:, None] <= column_limit[None, :])
        masked = jnp.where(valid_mask[None], scores, -1e+30)
        global_peak = lax.optimization_barrier(jnp.max(masked, axis=1))
        weights = jnp.exp(masked - global_peak[:, None, :])
        weight_total = lax.optimization_barrier(jnp.sum(weights, axis=1))
        weights16 = lax.optimization_barrier(weights.astype(jnp.bfloat16))
        numerator = jnp.einsum('ktc,tl->kcl', weights16.astype(jnp.float32), flat_rows[:, LATK:].astype(jnp.float32))
        context = lax.optimization_barrier((numerator / weight_total[..., None]).astype(jnp.bfloat16))
        result = jnp.einsum('kcl,lkd->kcd', context.astype(jnp.float32), value_heads.astype(jnp.float32)).astype(jnp.bfloat16)
        return result.reshape(KVH, STEPS, GROUP, HD_DIM).transpose(1, 0, 2, 3).reshape(STEPS, HEADS * HD_DIM)
    outputs = lax.map(one_request, jnp.arange(REQS, dtype=jnp.int32))
    attended = outputs.transpose(1, 0, 2)
    lane_count = N_HD * N_PF
    row_count = PG_DEV * REQS
    targets = page_target.reshape(N_CTX, lane_count, row_count)
    chosen = (targets[..., None] == jnp.arange(N_CTX, dtype=jnp.int32)).astype(jnp.int32)
    row_rank = lax.optimization_barrier(jnp.sum(jnp.cumsum(chosen, axis=2) * chosen, axis=3)) - 1
    sender = jnp.arange(N_CTX, dtype=jnp.int32)[:, None, None]
    lane_index = jnp.arange(lane_count, dtype=jnp.int32)[None, :, None]
    where_to = ((targets * lane_count + lane_index) * SLOTS + sender * CAP + row_rank).reshape(-1)
    flat_pages = latent_pages.reshape(N_CTX * lane_count * row_count, PAGE, LATK + LATV)
    stored_pages = jnp.zeros((N_CTX * lane_count * SLOTS, PAGE, LATK + LATV), jnp.bfloat16).at[where_to].set(flat_pages)
    return (attended, stored_pages)
```

```python
import functools
import math

import jax
import jax.numpy as jnp
import numpy as np
from jax import lax
from jax.experimental import pallas as pl
from jax.experimental.pallas import tpu as pltpu
from jax.sharding import PartitionSpec as P

KVH = 8
GROUP = 8
HD_DIM = 128
LATK = 256
LATV = 256
PAGE = 16
STEPS = 2
REQS = 8
COLS = STEPS * GROUP
LANES = 128
MESH = pl.DeviceIdType.MESH
NEVER = -1e30


def frequencies(head_width):
    exponent = np.arange(0, head_width, 2).astype(np.float32) / np.float32(head_width)
    inverse = np.power(np.float32(500000.0), -exponent).astype(np.float32)
    wavelength = np.float32(2.0 * math.pi) / inverse
    smooth = (np.float32(8192.0) / wavelength - np.float32(1.0)) / np.float32(3.0)
    mixed = (1.0 - smooth) * inverse / 8.0 + smooth * inverse
    return np.where(
        wavelength > 8192.0, inverse / 8.0, np.where(wavelength < 2048.0, inverse, mixed)
    ).astype(np.float32)


def iota(shape, dim):
    return lax.broadcasted_iota(jnp.int32, shape, dim)


def kernel(
    n_ctx, n_hd, n_pf, capacity,
    pages, targets, counts, lengths, queries, key_up, value_up, freqs,
    stored, attended,
    packed, source_v, source_s, turned, q_all, part, stats, precv, pstats,
    summed, sstats, zrecv, zstats, result, table,
    page_send, page_recv, own_sem, source_sem, q_send, q_recv,
    part_send, part_recv, pst_send, pst_recv, z_send, z_recv, zst_send, zst_recv,
    out_send, out_recv,
):
    ctx, hd, pf = lax.axis_index("ctx"), lax.axis_index("hd"), lax.axis_index("pf")
    page_rows = pages.shape[0]
    rows = page_rows * REQS
    tokens = page_rows * PAGE
    device = (ctx * n_hd + hd) * n_pf + pf
    local_heads = KVH // n_hd
    per_req = local_heads * COLS
    own_reqs = REQS // n_pf

    def at(axis, index, offset, size):
        return {axis: lax.rem(index + offset, size)}

    plane_offsets = [(a, b) for a in range(n_hd) for b in range(n_pf) if a or b]
    out_offsets = [(a, b) for a in range(n_ctx) for b in range(n_pf) if a or b]

    barrier = pltpu.get_barrier_semaphore()
    greeted = 0
    for a, b in out_offsets:
        pl.semaphore_signal(
            barrier, inc=1, device_id_type=MESH,
            device_id={**at("ctx", ctx, a, n_ctx), **at("pf", pf, b, n_pf)},
        )
        greeted += 1
    for a, b in plane_offsets:
        if a:
            pl.semaphore_signal(
                barrier, inc=1, device_id_type=MESH,
                device_id={**at("hd", hd, a, n_hd), **at("pf", pf, b, n_pf)},
            )
            greeted += 1

    target_row = targets[pl.ds(device, 1), :]
    down, across = iota((rows, rows), 0), iota((rows, rows), 1)
    spread = jnp.broadcast_to(target_row, (rows, rows))
    target_col = jnp.sum(jnp.where(down == across, spread, 0), axis=1, keepdims=True)
    earlier = jnp.where((spread == target_col) & (across < down), 1, 0)
    slot_col = target_col * capacity + jnp.sum(earlier, axis=1, keepdims=True)
    width = source_v.shape[1]
    hit = slot_col == iota((rows, width), 1)
    source_v[...] = (
        jnp.sum(jnp.where(hit, iota((rows, width), 0) + 1, 0), axis=0, keepdims=True) - 1
    )
    to_scalars = pltpu.make_async_copy(source_v, source_s, source_sem)
    to_scalars.start()
    to_scalars.wait()

    def pack(block):
        def one(index, _):
            slot = block * capacity + index
            row = source_s[0, slot]
            safe = jnp.maximum(row, 0)
            page = pages[lax.div(safe, REQS), lax.rem(safe, REQS)]
            packed[slot] = jnp.where(row >= 0, page, jnp.zeros_like(page))
            return 0

        lax.fori_loop(0, capacity, one, 0)

    def page_copy(offset):
        block = lax.rem(ctx + offset, n_ctx)
        return pltpu.make_async_remote_copy(
            src_ref=packed.at[pl.ds(block * capacity, capacity)],
            dst_ref=stored.at[pl.ds(ctx * capacity, capacity)],
            send_sem=page_send.at[offset],
            recv_sem=page_recv.at[offset],
            device_id=at("ctx", ctx, offset, n_ctx),
            device_id_type=MESH,
        )

    half = n_ctx // 2
    order = sorted(range(1, n_ctx), key=lambda k: (abs(k - half), -k))
    page_copies = [page_copy(k) for k in order]
    for position, k in enumerate(order):
        pack(lax.rem(ctx + k, n_ctx))
        if position == 0:
            pl.semaphore_wait(barrier, greeted)
        page_copies[position].start()
    pack(ctx)
    own_copy = pltpu.make_async_copy(
        packed.at[pl.ds(ctx * capacity, capacity)],
        stored.at[pl.ds(ctx * capacity, capacity)],
        own_sem,
    )
    own_copy.start()

    lane = iota((REQS, HD_DIM), 1)
    sublane = iota((REQS, HD_DIM), 0)
    sign = jnp.where(lane < HD_DIM // 2, -1.0, 1.0).astype(jnp.float32)
    first_position = jnp.zeros((REQS, HD_DIM), jnp.int32)
    for r in range(REQS):
        first_position = jnp.where(sublane == r, lengths[r], first_position)
    frequency = jnp.broadcast_to(freqs[...], (REQS, HD_DIM))
    for s in range(STEPS):
        angle = (first_position + s).astype(jnp.float32) * frequency
        cosine, sine = jnp.cos(angle), jnp.sin(angle) * sign
        for head in range(local_heads * GROUP):
            k, g = head // GROUP, head % GROUP
            values = queries[s, :, head * HD_DIM:(head + 1) * HD_DIM].astype(jnp.float32)
            row = k * COLS + s * GROUP + g
            turned[row * REQS:(row + 1) * REQS, :] = (
                values * cosine + pltpu.roll(values, HD_DIM // 2, 1) * sine
            )
    for r in range(REQS):
        q_all[0, r] = turned[pl.ds(r, per_req, stride=REQS), :].astype(jnp.bfloat16)
    q_copies = []
    for a in range(1, n_hd):
        q_copies.append(
            pltpu.make_async_remote_copy(
                src_ref=q_all.at[0], dst_ref=q_all.at[a],
                send_sem=q_send.at[a], recv_sem=q_recv.at[a],
                device_id=at("hd", hd, a, n_hd), device_id_type=MESH,
            )
        )
        q_copies[-1].start()

    token = iota((tokens, HD_DIM), 0)
    angle = (device * tokens + token).astype(jnp.float32) * jnp.broadcast_to(
        freqs[...], (tokens, HD_DIM)
    )
    table[0] = jnp.cos(angle)
    table[1] = jnp.sin(angle) * jnp.where(iota((tokens, HD_DIM), 1) < HD_DIM // 2, -1.0, 1.0)

    own_counts = counts[pl.ds(pl.multiple_of(device * page_rows, page_rows), page_rows), :]
    pick = (iota((page_rows, tokens), 1) // PAGE == iota((page_rows, tokens), 0))
    spread_counts = lax.dot_general(
        own_counts.astype(jnp.float32).astype(jnp.bfloat16),
        jnp.where(pick, 1.0, 0.0).astype(jnp.bfloat16),
        (((0,), (0,)), ((), ())),
        preferred_element_type=jnp.float32,
    )
    column = iota((COLS, tokens), 1)
    step_of = iota((COLS, tokens), 0) // GROUP
    inside = (column % PAGE).astype(jnp.float32)
    position = device * tokens + column
    square = iota((LANES, LANES), 0) == iota((LANES, LANES), 1)
    request_of = iota((REQS, tokens), 0)

    for copy in q_copies:
        copy.wait()

    def attend(r, _):
        latent = pages[:, r].reshape(tokens, LATK + LATV)
        key_latent, value_latent = latent[:, :LATK], latent[:, LATK:]
        filled = jnp.sum(jnp.where(request_of == r, spread_counts, 0.0), axis=0, keepdims=True)
        valid = (inside < filled) & (position <= lengths[r] + step_of)
        peaks, totals = [], []
        for a in range(n_hd):
            owner = lax.rem(hd + n_hd - a, n_hd)
            for k in range(local_heads):
                start = pl.multiple_of((owner * local_heads + k) * HD_DIM, HD_DIM)
                rebuilt = jnp.dot(
                    key_latent, key_up[:, pl.ds(start, HD_DIM)],
                    preferred_element_type=jnp.float32,
                )
                keys = (
                    rebuilt * table[0] + pltpu.roll(rebuilt, HD_DIM // 2, 1) * table[1]
                ).astype(jnp.bfloat16)
                scores = lax.dot_general(
                    q_all[a, r, k * COLS:(k + 1) * COLS, :], keys,
                    (((1,), (1,)), ((), ())), preferred_element_type=jnp.float32,
                ) * (1.0 / math.sqrt(HD_DIM))
                masked = jnp.where(valid, scores, NEVER)
                peak = jnp.max(masked, axis=1, keepdims=True)
                weights = jnp.where(valid, jnp.exp(masked - peak), 0.0)
                peaks.append(peak)
                totals.append(jnp.sum(weights, axis=1, keepdims=True))
                part[a, r, k * COLS:(k + 1) * COLS, :] = jnp.dot(
                    weights.astype(jnp.bfloat16), value_latent,
                    preferred_element_type=jnp.float32,
                ).astype(jnp.bfloat16)
        for index, pieces in enumerate((peaks, totals)):
            tall = jnp.concatenate(pieces, axis=0)
            stats[index, pl.ds(r, 1), :] = jnp.sum(
                jnp.where(square, tall, 0.0), axis=0, keepdims=True
            )
        return 0

    lax.fori_loop(0, REQS, attend, 0)

    plane = []
    for a, b in plane_offsets:
        slot = a * n_pf + b
        there = {**at("hd", hd, a, n_hd), **at("pf", pf, b, n_pf)}
        other = lax.rem(pf + b, n_pf)
        mine = (n_hd - a) % n_hd
        plane.append(
            pltpu.make_async_remote_copy(
                src_ref=part.at[mine, pl.ds(other * own_reqs, own_reqs)],
                dst_ref=precv.at[slot],
                send_sem=part_send.at[slot], recv_sem=part_recv.at[slot],
                device_id=there, device_id_type=MESH,
            )
        )
        plane.append(
            pltpu.make_async_remote_copy(
                src_ref=stats, dst_ref=pstats.at[slot],
                send_sem=pst_send.at[slot], recv_sem=pst_recv.at[slot],
                device_id=there, device_id_type=MESH,
            )
        )
    for copy in plane:
        copy.start()
    for copy in plane:
        copy.wait()

    def to_column(row, shift):
        there = iota((per_req, LANES), 1) == iota((per_req, LANES), 0) + shift
        return jnp.sum(
            jnp.where(there, jnp.broadcast_to(row, (per_req, LANES)), 0.0),
            axis=1, keepdims=True,
        )

    sources = [(0, 0)] + plane_offsets
    for q in range(own_reqs):
        request = pf * own_reqs + q
        peaks, totals, numerators = [], [], []
        for a, b in sources:
            slot = a * n_pf + b
            shift = ((n_hd - a) % n_hd) * per_req
            if slot:
                rows_of = (pstats[slot, 0, pl.ds(request, 1), :], pstats[slot, 1, pl.ds(request, 1), :])
                numerators.append(precv[slot, q])
            else:
                rows_of = (stats[0, pl.ds(request, 1), :], stats[1, pl.ds(request, 1), :])
                numerators.append(part[0, request])
            peaks.append(to_column(rows_of[0], shift))
            totals.append(to_column(rows_of[1], shift))
        top = functools.reduce(jnp.maximum, peaks)
        total = jnp.zeros_like(top)
        numerator = jnp.zeros((per_req, LATV), jnp.float32)
        for peak, part_total, piece in zip(peaks, totals, numerators):
            factor = jnp.exp(peak - top)
            total = total + factor * part_total
            numerator = numerator + factor * piece.astype(jnp.float32)
        summed[q] = numerator.astype(jnp.bfloat16)
        corner = iota((per_req, LANES), 0) == iota((per_req, LANES), 1)
        for index, tall in enumerate((top, total)):
            sstats[index, q:q + 1, :] = jnp.sum(
                jnp.where(corner, tall, 0.0), axis=0, keepdims=True
            )

    def if_owner(index, body):
        if own_reqs >= n_ctx:
            body()
        else:
            pl.when(index < own_reqs)(body)

    def z_copies(offset):
        there = at("ctx", ctx, offset, n_ctx)
        other = lax.rem(ctx + offset, n_ctx)
        if own_reqs < n_ctx:
            other = jnp.minimum(other, own_reqs - 1)
        return (
            pltpu.make_async_remote_copy(
                src_ref=summed.at[other], dst_ref=zrecv.at[offset],
                send_sem=z_send.at[offset], recv_sem=z_recv.at[offset],
                device_id=there, device_id_type=MESH,
            ),
            pltpu.make_async_remote_copy(
                src_ref=sstats, dst_ref=zstats.at[offset],
                send_sem=zst_send.at[offset], recv_sem=zst_recv.at[offset],
                device_id=there, device_id_type=MESH,
            ),
        )

    def out_copy(a, b):
        slot = a * n_pf + b
        return pltpu.make_async_remote_copy(
            src_ref=result.at[pf, ctx], dst_ref=result.at[pf, ctx],
            send_sem=out_send.at[slot], recv_sem=out_recv.at[slot],
            device_id={**at("ctx", ctx, a, n_ctx), **at("pf", pf, b, n_pf)},
            device_id_type=MESH,
        )

    for offset in range(1, n_ctx):
        def start(offset=offset):
            for copy in z_copies(offset):
                copy.start()
        if_owner(lax.rem(ctx + offset, n_ctx), start)

    def finish():
        for offset in range(1, n_ctx):
            for copy in z_copies(offset):
                copy.wait_recv()
        peaks = [to_column(sstats[0, pl.ds(ctx, 1), :], 0)]
        totals = [to_column(sstats[1, pl.ds(ctx, 1), :], 0)]
        numerators = [summed[ctx]]
        for offset in range(1, n_ctx):
            peaks.append(to_column(zstats[offset, 0, pl.ds(ctx, 1), :], 0))
            totals.append(to_column(zstats[offset, 1, pl.ds(ctx, 1), :], 0))
            numerators.append(zrecv[offset])
        top = functools.reduce(jnp.maximum, peaks)
        total = jnp.zeros_like(top)
        numerator = jnp.zeros((per_req, LATV), jnp.float32)
        for peak, part_total, piece in zip(peaks, totals, numerators):
            factor = jnp.exp(peak - top)
            total = total + factor * part_total
            numerator = numerator + factor * piece.astype(jnp.float32)
        context = (numerator / total).astype(jnp.bfloat16)
        for k in range(local_heads):
            result[pf, ctx, k * COLS:(k + 1) * COLS, :] = jnp.dot(
                context[k * COLS:(k + 1) * COLS],
                value_up[:, k * HD_DIM:(k + 1) * HD_DIM],
                preferred_element_type=jnp.float32,
            ).astype(jnp.bfloat16)
        for a, b in out_offsets:
            out_copy(a, b).start()

    if_owner(ctx, finish)
    for offset in range(1, n_ctx):
        def sent(offset=offset):
            for copy in z_copies(offset):
                copy.wait_send()
        if_owner(lax.rem(ctx + offset, n_ctx), sent)
    for a, b in out_offsets:
        def arrived(a=a, b=b):
            out_copy(a, b).wait_recv()
        if_owner(lax.rem(ctx + n_ctx - a, n_ctx), arrived)

    def left():
        for a, b in out_offsets:
            out_copy(a, b).wait_send()

    if_owner(ctx, left)
    attended[...] = result[:, :own_reqs]
    own_copy.wait()
    for copy in page_copies:
        copy.wait()


def on_device(latent_pages, page_target, page_count, context_length, queries, key_up, value_up):
    n_ctx, n_hd, n_pf = lax.axis_size("ctx"), lax.axis_size("hd"), lax.axis_size("pf")
    page_rows, request_count, page_length, latent_width = latent_pages.shape
    row_count = page_rows * request_count
    capacity = max(2, 9 * row_count // (8 * n_ctx))
    slot_count = n_ctx * capacity
    local_heads = KVH // n_hd
    per_req = local_heads * COLS
    own_reqs = REQS // n_pf
    n_plane = n_hd * n_pf
    targets = page_target.reshape(-1, row_count)
    half = frequencies(HD_DIM)
    freqs = jnp.asarray(np.concatenate([half, half])[None, :])
    vmem = pl.BlockSpec(memory_space=pltpu.VMEM)
    dma = pltpu.SemaphoreType.DMA
    stored, rows = pl.pallas_call(
        functools.partial(kernel, n_ctx, n_hd, n_pf, capacity),
        out_shape=(
            jax.ShapeDtypeStruct((slot_count, page_length, latent_width), jnp.bfloat16),
            jax.ShapeDtypeStruct((n_pf, own_reqs, per_req, HD_DIM), jnp.bfloat16),
        ),
        in_specs=[
            vmem, vmem, vmem, pl.BlockSpec(memory_space=pltpu.SMEM), vmem, vmem, vmem, vmem,
        ],
        out_specs=(pl.BlockSpec(memory_space=pl.ANY), vmem),
        scratch_shapes=[
            pltpu.VMEM((slot_count, page_length, latent_width), jnp.bfloat16),
            pltpu.VMEM((1, -(-slot_count // LANES) * LANES), jnp.int32),
            pltpu.SMEM((1, -(-slot_count // LANES) * LANES), jnp.int32),
            pltpu.VMEM((per_req * REQS, HD_DIM), jnp.float32),
            pltpu.VMEM((n_hd, REQS, per_req, HD_DIM), jnp.bfloat16),
            pltpu.VMEM((n_hd, REQS, per_req, LATV), jnp.bfloat16),
            pltpu.VMEM((2, REQS, LANES), jnp.float32),
            pltpu.VMEM((n_plane, own_reqs, per_req, LATV), jnp.bfloat16),
            pltpu.VMEM((n_plane, 2, REQS, LANES), jnp.float32),
            pltpu.VMEM((own_reqs, per_req, LATV), jnp.bfloat16),
            pltpu.VMEM((2, own_reqs, LANES), jnp.float32),
            pltpu.VMEM((n_ctx, per_req, LATV), jnp.bfloat16),
            pltpu.VMEM((n_ctx, 2, own_reqs, LANES), jnp.float32),
            pltpu.VMEM((n_pf, n_ctx, per_req, HD_DIM), jnp.bfloat16),
            pltpu.VMEM((2, page_rows * PAGE, HD_DIM), jnp.float32),
            dma((n_ctx,)), dma((n_ctx,)), dma, dma, dma((n_hd,)), dma((n_hd,)),
            dma((n_plane,)), dma((n_plane,)), dma((n_plane,)), dma((n_plane,)),
            dma((n_ctx,)), dma((n_ctx,)), dma((n_ctx,)), dma((n_ctx,)),
            dma((n_ctx * n_pf,)), dma((n_ctx * n_pf,)),
        ],
        compiler_params=pltpu.CompilerParams(
            collective_id=0, has_side_effects=True, vmem_limit_bytes=40 * 1024 * 1024
        ),
    )(latent_pages, targets, page_count, context_length, queries, key_up, value_up, freqs)
    attended = (
        rows.reshape(REQS, local_heads, STEPS, GROUP, HD_DIM)
        .transpose(2, 0, 1, 3, 4)
        .reshape(STEPS, REQS, local_heads * GROUP * HD_DIM)
    )
    return (attended, stored)


def solution(mesh):
    placed = (
        P(("ctx", "hd", "pf"), "grp", None, None),
        P(None, "grp", None),
        P(None, "grp"),
        P("grp"),
        P(None, "grp", "hd"),
        P(),
        P(None, "hd"),
    )
    return jax.shard_map(
        on_device,
        mesh=mesh,
        in_specs=placed,
        out_specs=(P(None, "grp", "hd"), P(("grp", "ctx", "hd", "pf"), None, None)),
        check_vma=False,
    )
```

```python
import functools
import math

import jax
import jax.numpy as jnp
import numpy as np
from jax import lax
from jax.experimental import pallas as pl
from jax.experimental.pallas import tpu as pltpu
from jax.sharding import PartitionSpec as P

KVH = 8
GROUP = 8
HD_DIM = 128
LATK = 256
LATV = 256
PAGE = 16
STEPS = 2
REQS = 8
COLS = STEPS * GROUP
LANES = 128
MESH = pl.DeviceIdType.MESH
NEVER = -1e30
EARLY, LATE, NEAR = 36, 6, 18


def frequencies(head_width):
    exponent = np.arange(0, head_width, 2).astype(np.float32) / np.float32(head_width)
    inverse = np.power(np.float32(500000.0), -exponent).astype(np.float32)
    wavelength = np.float32(2.0 * math.pi) / inverse
    smooth = (np.float32(8192.0) / wavelength - np.float32(1.0)) / np.float32(3.0)
    mixed = (1.0 - smooth) * inverse / 8.0 + smooth * inverse
    return np.where(
        wavelength > 8192.0, inverse / 8.0, np.where(wavelength < 2048.0, inverse, mixed)
    ).astype(np.float32)


def iota(shape, dim):
    return lax.broadcasted_iota(jnp.int32, shape, dim)


def kernel(
    n_ctx, n_hd, n_pf, capacity,
    pages_h, targets_h, counts_h, lengths_h, queries_h, key_up_h, value_up_h, freqs_h,
    stored, attended,
    pages, targets, counts, lengths, queries, key_up, value_up, freqs,
    packed, source_v, source_s, turned, q_all, part, stats, precv, pstats,
    summed, sstats, zrecv, zstats, result, table,
    in_sem, page_send, page_recv, own_sem, source_sem, q_send, q_recv,
    part_send, part_recv, pst_send, pst_recv, z_send, z_recv, zst_send, zst_recv,
    out_send, out_recv, fwd_send, fwd_recv,
):
    ctx, hd, pf = lax.axis_index("ctx"), lax.axis_index("hd"), lax.axis_index("pf")
    page_rows = pages.shape[0]
    rows = page_rows * REQS
    tokens = page_rows * PAGE
    device = (ctx * n_hd + hd) * n_pf + pf
    local_heads = KVH // n_hd
    per_req = local_heads * COLS
    own_reqs = REQS // n_pf
    plane_offsets = [(a, b) for a in range(n_hd) for b in range(n_pf) if a or b]

    def at(axis, index, offset, size):
        return {axis: lax.rem(index + offset, size)}

    barrier = pltpu.get_barrier_semaphore()
    for x in range(1, n_ctx):
        pl.semaphore_signal(barrier, inc=1, device_id_type=MESH, device_id={"ctx": ctx ^ x})
    for a, b in plane_offsets:
        pl.semaphore_signal(
            barrier, inc=1, device_id_type=MESH,
            device_id={**at("hd", hd, a, n_hd), **at("pf", pf, b, n_pf)},
        )
    greeted = n_ctx - 1 + len(plane_offsets)

    loads = [
        pltpu.make_async_copy(there, here, in_sem.at[index])
        for index, (there, here) in enumerate((
            (targets_h, targets), (pages_h, pages), (lengths_h, lengths), (freqs_h, freqs),
            (queries_h, queries), (counts_h, counts), (key_up_h, key_up),
            (value_up_h, value_up),
        ))
    ]
    for load in loads:
        load.start()
    loads[0].wait()

    total_pages = targets.shape[2]
    tall = jnp.concatenate([targets[r] for r in range(REQS)] * page_rows, axis=0)
    own_page = iota((rows, total_pages), 0) // REQS + device * page_rows
    target_col = jnp.sum(
        jnp.where(iota((rows, total_pages), 1) == own_page, tall, 0), axis=1, keepdims=True
    )
    down, across = iota((rows, rows), 0), iota((rows, rows), 1)
    target_row = jnp.sum(jnp.where(down == across, target_col, 0), axis=0, keepdims=True)
    earlier = jnp.where((target_row == target_col) & (across < down), 1, 0)
    slot_col = target_col * capacity + jnp.sum(earlier, axis=1, keepdims=True)
    width = source_v.shape[1]
    hit = slot_col == iota((rows, width), 1)
    source_v[...] = (
        jnp.sum(jnp.where(hit, iota((rows, width), 0) + 1, 0), axis=0, keepdims=True) - 1
    )
    to_scalars = pltpu.make_async_copy(source_v, source_s, source_sem)
    to_scalars.start()
    to_scalars.wait()
    loads[1].wait()

    def pack(block):
        def one(index, _):
            slot = block * capacity + index
            row = source_s[0, slot]
            safe = jnp.maximum(row, 0)
            page = pages[lax.div(safe, REQS), lax.rem(safe, REQS)]
            packed[slot] = jnp.where(row >= 0, page, jnp.zeros_like(page))
            return 0

        lax.fori_loop(0, capacity, one, 0)

    order = list(range(n_ctx // 2, n_ctx)) + list(range(1, n_ctx // 2))
    early, late, near = order[:n_ctx // 4], order[n_ctx // 4:n_ctx // 2], order[n_ctx // 2:]
    cuts = (EARLY * capacity // 36, LATE * capacity // 36, NEAR * capacity // 36)
    pieces = (
        [(x, 0, cuts[0]) for x in early] + [(x, 0, cuts[2]) for x in near],
        [(x, cuts[0], capacity) for x in early] + [(x, 0, cuts[1]) for x in late],
        [(x, cuts[1], capacity) for x in late] + [(x, cuts[2], capacity) for x in near],
    )
    page_copies = []

    def send_pages(stage):
        for x, low, high in pieces[stage]:
            if low == high:
                continue
            block = ctx ^ x
            slot = 2 * x + (1 if low else 0)
            copy = pltpu.make_async_remote_copy(
                src_ref=packed.at[pl.ds(block * capacity + low, high - low)],
                dst_ref=stored.at[pl.ds(ctx * capacity + low, high - low)],
                send_sem=page_send.at[slot],
                recv_sem=page_recv.at[slot],
                device_id={"ctx": block},
                device_id_type=MESH,
            )
            copy.start()
            page_copies.append(copy)

    for x in early + near:
        pack(ctx ^ x)
    pl.semaphore_wait(barrier, greeted)
    send_pages(0)
    for x in late:
        pack(ctx ^ x)
    pack(ctx)
    own_copy = pltpu.make_async_copy(
        packed.at[pl.ds(ctx * capacity, capacity)],
        stored.at[pl.ds(ctx * capacity, capacity)],
        own_sem,
    )
    own_copy.start()

    for load in loads[2:]:
        load.wait()
    lane = iota((REQS, HD_DIM), 1)
    sublane = iota((REQS, HD_DIM), 0)
    sign = jnp.where(lane < HD_DIM // 2, -1.0, 1.0).astype(jnp.float32)
    first_position = jnp.zeros((REQS, HD_DIM), jnp.int32)
    for r in range(REQS):
        first_position = jnp.where(sublane == r, lengths[r], first_position)
    frequency = jnp.broadcast_to(freqs[...], (REQS, HD_DIM))
    for s in range(STEPS):
        angle = (first_position + s).astype(jnp.float32) * frequency
        cosine, sine = jnp.cos(angle), jnp.sin(angle) * sign
        for head in range(local_heads * GROUP):
            k, g = head // GROUP, head % GROUP
            values = queries[s, :, head * HD_DIM:(head + 1) * HD_DIM].astype(jnp.float32)
            row = k * COLS + s * GROUP + g
            turned[row * REQS:(row + 1) * REQS, :] = (
                values * cosine + pltpu.roll(values, HD_DIM // 2, 1) * sine
            )
    for r in range(REQS):
        q_all[0, r] = turned[pl.ds(r, per_req, stride=REQS), :].astype(jnp.bfloat16)
    q_copies = []
    for a in range(1, n_hd):
        q_copies.append(
            pltpu.make_async_remote_copy(
                src_ref=q_all.at[0], dst_ref=q_all.at[a],
                send_sem=q_send.at[a], recv_sem=q_recv.at[a],
                device_id=at("hd", hd, a, n_hd), device_id_type=MESH,
            )
        )
        q_copies[-1].start()

    token = iota((tokens, HD_DIM), 0)
    angle = (device * tokens + token).astype(jnp.float32) * jnp.broadcast_to(
        freqs[...], (tokens, HD_DIM)
    )
    table[0] = jnp.cos(angle)
    table[1] = jnp.sin(angle) * jnp.where(iota((tokens, HD_DIM), 1) < HD_DIM // 2, -1.0, 1.0)

    pick = iota((total_pages, tokens), 0) == iota((total_pages, tokens), 1) // PAGE + device * page_rows
    spread_counts = jnp.dot(
        counts[...].astype(jnp.float32).astype(jnp.bfloat16),
        jnp.where(pick, 1.0, 0.0).astype(jnp.bfloat16),
        preferred_element_type=jnp.float32,
    )
    all_cols = KVH * COLS
    column = iota((all_cols, tokens), 1)
    step_of = iota((all_cols, tokens), 0) // GROUP % STEPS
    inside = (iota((1, tokens), 1) % PAGE).astype(jnp.float32)
    reach = device * tokens + column - step_of
    square = iota((LANES, LANES), 0) == iota((LANES, LANES), 1)
    request_of = iota((REQS, tokens), 0)

    for copy in q_copies:
        copy.wait()

    def part_copy(a, b, q):
        slot = a * n_pf + b
        other = lax.rem(pf + b, n_pf)
        return pltpu.make_async_remote_copy(
            src_ref=part.at[(n_hd - a) % n_hd, other * own_reqs + q],
            dst_ref=precv.at[slot, q],
            send_sem=part_send.at[slot, q], recv_sem=part_recv.at[slot, q],
            device_id={**at("hd", hd, a, n_hd), **at("pf", pf, b, n_pf)},
            device_id_type=MESH,
        )

    def attend(b, q):
        r = lax.rem(pf + b, n_pf) * own_reqs + q
        latent = pages[:, r].reshape(tokens, LATK + LATV)
        key_latent, value_latent = latent[:, :LATK], latent[:, LATK:]
        filled = jnp.sum(jnp.where(request_of == r, spread_counts, 0.0), axis=0, keepdims=True)
        valid = (inside < filled) & (reach <= lengths[r])
        scores = []
        for a in range(n_hd):
            owner = lax.rem(hd + n_hd - a, n_hd)
            start = pl.multiple_of(owner * local_heads * HD_DIM, HD_DIM)
            rebuilt = jnp.dot(
                key_latent, key_up[:, pl.ds(start, local_heads * HD_DIM)],
                preferred_element_type=jnp.float32,
            )
            for k in range(local_heads):
                plain = rebuilt[:, k * HD_DIM:(k + 1) * HD_DIM]
                keys = (
                    plain * table[0] + pltpu.roll(plain, HD_DIM // 2, 1) * table[1]
                ).astype(jnp.bfloat16)
                scores.append(lax.dot_general(
                    q_all[a, r, k * COLS:(k + 1) * COLS, :], keys,
                    (((1,), (1,)), ((), ())), preferred_element_type=jnp.float32,
                ))
        scores = jnp.concatenate(scores, axis=0) * (1.0 / math.sqrt(HD_DIM))
        masked = jnp.where(valid, scores, NEVER)
        peak = jnp.max(masked, axis=1, keepdims=True)
        weights = jnp.where(valid, jnp.exp(masked - peak), 0.0)
        total = jnp.sum(weights, axis=1, keepdims=True)
        numerator = jnp.dot(
            weights.astype(jnp.bfloat16), value_latent, preferred_element_type=jnp.float32
        ).astype(jnp.bfloat16)
        for a in range(n_hd):
            part[a, r] = numerator[a * per_req:(a + 1) * per_req]
            if a or b:
                part_copy((n_hd - a) % n_hd, b, q).start()
        for index, tall in enumerate((peak, total)):
            stats[index, pl.ds(r, 1), :] = jnp.sum(
                jnp.where(square, tall, 0.0), axis=0, keepdims=True
            )

    for b in list(range(1, n_pf)) + [0]:
        def one_request(q, _, b=b):
            attend(b, q)
            return 0

        lax.fori_loop(0, own_reqs, one_request, 0)

    plane = [
        pltpu.make_async_remote_copy(
            src_ref=stats, dst_ref=pstats.at[a * n_pf + b],
            send_sem=pst_send.at[a * n_pf + b], recv_sem=pst_recv.at[a * n_pf + b],
            device_id={**at("hd", hd, a, n_hd), **at("pf", pf, b, n_pf)},
            device_id_type=MESH,
        )
        for a, b in plane_offsets
    ]
    for copy in plane:
        copy.start()
    for copy in plane:
        copy.wait()

    def to_column(row, shift):
        there = iota((per_req, LANES), 1) == iota((per_req, LANES), 0) + shift
        return jnp.sum(
            jnp.where(there, jnp.broadcast_to(row, (per_req, LANES)), 0.0),
            axis=1, keepdims=True,
        )

    def merge(peaks, totals, numerators):
        top = functools.reduce(jnp.maximum, peaks)
        total = jnp.zeros_like(top)
        numerator = jnp.zeros(numerators[0].shape, jnp.float32)
        for peak, part_total, piece in zip(peaks, totals, numerators):
            factor = jnp.exp(peak - top)
            total = total + factor * part_total
            numerator = numerator + factor * piece.astype(jnp.float32)
        return top, total, numerator

    for q in range(own_reqs):
        request = pf * own_reqs + q
        for a, b in plane_offsets:
            part_copy(a, b, q).wait()
        peaks, totals, numerators = [], [], []
        for a, b in [(0, 0)] + plane_offsets:
            slot = a * n_pf + b
            shift = ((n_hd - a) % n_hd) * per_req
            if slot:
                pair = (pstats[slot, 0, pl.ds(request, 1), :], pstats[slot, 1, pl.ds(request, 1), :])
                numerators.append(precv[slot, q])
            else:
                pair = (stats[0, pl.ds(request, 1), :], stats[1, pl.ds(request, 1), :])
                numerators.append(part[0, request])
            peaks.append(to_column(pair[0], shift))
            totals.append(to_column(pair[1], shift))
        top, total, numerator = merge(peaks, totals, numerators)
        numerator = numerator.astype(jnp.bfloat16)
        for k in range(local_heads):
            summed[q, k * COLS:(k + 1) * COLS, :] = jnp.dot(
                numerator[k * COLS:(k + 1) * COLS],
                value_up[:, k * HD_DIM:(k + 1) * HD_DIM],
                preferred_element_type=jnp.float32,
            ).astype(jnp.bfloat16)
        corner = iota((per_req, LANES), 0) == iota((per_req, LANES), 1)
        for index, tall in enumerate((top, total)):
            sstats[index, q:q + 1, :] = jnp.sum(
                jnp.where(corner, tall, 0.0), axis=0, keepdims=True
            )

    def if_owner(index, body):
        if own_reqs >= n_ctx:
            body()
        else:
            pl.when(index < own_reqs)(body)

    def z_copies(x):
        other = ctx ^ x
        mine = other if own_reqs >= n_ctx else jnp.minimum(other, own_reqs - 1)
        return (
            pltpu.make_async_remote_copy(
                src_ref=summed.at[mine], dst_ref=zrecv.at[x],
                send_sem=z_send.at[x], recv_sem=z_recv.at[x],
                device_id={"ctx": other}, device_id_type=MESH,
            ),
            pltpu.make_async_remote_copy(
                src_ref=sstats, dst_ref=zstats.at[x],
                send_sem=zst_send.at[x], recv_sem=zst_recv.at[x],
                device_id={"ctx": other}, device_id_type=MESH,
            ),
        )

    def out_copy(x, came):
        owner = ctx ^ x if came else ctx
        return pltpu.make_async_remote_copy(
            src_ref=result.at[pf, owner], dst_ref=result.at[pf, owner],
            send_sem=out_send.at[x], recv_sem=out_recv.at[x],
            device_id={"ctx": ctx ^ x}, device_id_type=MESH,
        )

    def forward(x, b, came):
        place = lax.rem(pf + n_pf - b, n_pf) if came else pf
        slot = (b - 1) * n_ctx + x
        return pltpu.make_async_remote_copy(
            src_ref=result.at[place, ctx ^ x], dst_ref=result.at[place, ctx ^ x],
            send_sem=fwd_send.at[slot], recv_sem=fwd_recv.at[slot],
            device_id=at("pf", pf, b, n_pf), device_id_type=MESH,
        )

    for x in order:
        def start(x=x):
            for copy in z_copies(x):
                copy.start()
        if_owner(ctx ^ x, start)
    send_pages(1)

    def finish():
        for x in range(1, n_ctx):
            for copy in z_copies(x):
                copy.wait_recv()
        peaks = [to_column(sstats[0, pl.ds(ctx, 1), :], 0)]
        totals = [to_column(sstats[1, pl.ds(ctx, 1), :], 0)]
        numerators = [summed[ctx]]
        for x in range(1, n_ctx):
            peaks.append(to_column(zstats[x, 0, pl.ds(ctx, 1), :], 0))
            totals.append(to_column(zstats[x, 1, pl.ds(ctx, 1), :], 0))
            numerators.append(zrecv[x])
        top, total, numerator = merge(peaks, totals, numerators)
        result[pf, ctx] = (numerator / total).astype(jnp.bfloat16)
        for x in order:
            out_copy(x, False).start()
        for b in range(1, n_pf):
            forward(0, b, False).start()

    if_owner(ctx, finish)
    send_pages(2)
    for x in range(1, n_ctx):
        def passed_on(x=x):
            out_copy(x, True).wait_recv()
            for b in range(1, n_pf):
                forward(x, b, False).start()
        if_owner(ctx ^ x, passed_on)
    for x in range(n_ctx):
        def arrived(x=x):
            for b in range(1, n_pf):
                forward(x, b, True).wait_recv()
                forward(x, b, False).wait_send()
            if x:
                for copy in z_copies(x):
                    copy.wait_send()
        if_owner(ctx ^ x, arrived)

    def left():
        for x in range(1, n_ctx):
            out_copy(x, False).wait_send()

    if_owner(ctx, left)
    attended[...] = result[:, :own_reqs]
    own_copy.wait()
    for copy in page_copies:
        copy.wait()


def on_device(latent_pages, page_target, page_count, context_length, queries, key_up, value_up):
    n_ctx, n_hd, n_pf = lax.axis_size("ctx"), lax.axis_size("hd"), lax.axis_size("pf")
    page_rows, request_count, page_length, latent_width = latent_pages.shape
    row_count = page_rows * request_count
    capacity = max(2, 9 * row_count // (8 * n_ctx))
    slot_count = n_ctx * capacity
    slot_lanes = -(-slot_count // LANES) * LANES
    local_heads = KVH // n_hd
    per_req = local_heads * COLS
    own_reqs = REQS // n_pf
    n_plane = n_hd * n_pf
    half = frequencies(HD_DIM)
    operands = (
        latent_pages, page_target.transpose(1, 2, 0), page_count.T, context_length,
        queries, key_up, value_up, jnp.asarray(np.concatenate([half, half])[None, :]),
    )
    hbm = pl.BlockSpec(memory_space=pltpu.HBM)
    bf16, f32 = jnp.bfloat16, jnp.float32
    vmem, dma = pltpu.VMEM, pltpu.SemaphoreType.DMA
    stored, rows = pl.pallas_call(
        functools.partial(kernel, n_ctx, n_hd, n_pf, capacity),
        out_shape=(
            jax.ShapeDtypeStruct((slot_count, page_length, latent_width), bf16),
            jax.ShapeDtypeStruct((n_pf, own_reqs, per_req, HD_DIM), bf16),
        ),
        in_specs=[hbm] * len(operands),
        out_specs=(pl.BlockSpec(memory_space=pl.ANY), pl.BlockSpec(memory_space=pltpu.VMEM)),
        scratch_shapes=[
            (pltpu.SMEM if index == 3 else vmem)(operand.shape, operand.dtype)
            for index, operand in enumerate(operands)
        ] + [
            vmem((slot_count, page_length, latent_width), bf16),
            vmem((1, slot_lanes), jnp.int32),
            pltpu.SMEM((1, slot_lanes), jnp.int32),
            vmem((per_req * REQS, HD_DIM), f32),
            vmem((n_hd, REQS, per_req, HD_DIM), bf16),
            vmem((n_hd, REQS, per_req, LATV), bf16),
            vmem((2, REQS, LANES), f32),
            vmem((n_plane, own_reqs, per_req, LATV), bf16),
            vmem((n_plane, 2, REQS, LANES), f32),
            vmem((own_reqs, per_req, HD_DIM), bf16),
            vmem((2, own_reqs, LANES), f32),
            vmem((n_ctx, per_req, HD_DIM), bf16),
            vmem((n_ctx, 2, own_reqs, LANES), f32),
            vmem((n_pf, n_ctx, per_req, HD_DIM), bf16),
            vmem((2, page_rows * PAGE, HD_DIM), f32),
            dma((len(operands),)),
            dma((2 * n_ctx,)), dma((2 * n_ctx,)), dma, dma, dma((n_hd,)), dma((n_hd,)),
            dma((n_plane, own_reqs)), dma((n_plane, own_reqs)), dma((n_plane,)), dma((n_plane,)),
            dma((n_ctx,)), dma((n_ctx,)), dma((n_ctx,)), dma((n_ctx,)),
            dma((n_ctx,)), dma((n_ctx,)), dma((n_ctx * n_pf,)), dma((n_ctx * n_pf,)),
        ],
        compiler_params=pltpu.CompilerParams(
            collective_id=0, has_side_effects=True, vmem_limit_bytes=58 * 1024 * 1024
        ),
    )(*operands)
    attended = (
        rows.reshape(REQS, local_heads, STEPS, GROUP, HD_DIM)
        .transpose(2, 0, 1, 3, 4)
        .reshape(STEPS, REQS, local_heads * GROUP * HD_DIM)
    )
    return (attended, stored)


def solution(mesh):
    placed = (
        P(("ctx", "hd", "pf"), "grp", None, None),
        P(None, "grp", None),
        P(None, "grp"),
        P("grp"),
        P(None, "grp", "hd"),
        P(),
        P(None, "hd"),
    )
    return jax.shard_map(
        on_device,
        mesh=mesh,
        in_specs=placed,
        out_specs=(P(None, "grp", "hd"), P(("grp", "ctx", "hd", "pf"), None, None)),
        check_vma=False,
    )
```

```python
import functools
import math

import jax
import jax.numpy as jnp
import numpy as np
from jax import lax
from jax.experimental import pallas as pl
from jax.experimental.pallas import tpu as pltpu
from jax.sharding import PartitionSpec as P

KVH = 8
GROUP = 8
HD_DIM = 128
LATK = 256
LATV = 256
PAGE = 16
STEPS = 2
REQS = 8
COLS = STEPS * GROUP
LANES = 128
MESH = pl.DeviceIdType.MESH
NEVER = -1e30
SPLITS = 8
EARLY, LATE, NEAR = 36, 6, 18


def frequencies(head_width):
    exponent = np.arange(0, head_width, 2).astype(np.float32) / np.float32(head_width)
    inverse = np.power(np.float32(500000.0), -exponent).astype(np.float32)
    wavelength = np.float32(2.0 * math.pi) / inverse
    smooth = (np.float32(8192.0) / wavelength - np.float32(1.0)) / np.float32(3.0)
    mixed = (1.0 - smooth) * inverse / 8.0 + smooth * inverse
    return np.where(
        wavelength > 8192.0, inverse / 8.0, np.where(wavelength < 2048.0, inverse, mixed)
    ).astype(np.float32)


def iota(shape, dim):
    return lax.broadcasted_iota(jnp.int32, shape, dim)


def kernel(
    n_ctx, n_hd, n_pf, capacity,
    pages_h, targets_h, counts_h, lengths_h, queries_h, key_up_h, value_up_h, freqs_h,
    stored, attended,
    pages, targets, counts, lengths, queries, key_up, value_up, freqs,
    packed, source_v, source_s, turned, q_all, part, stats, precv, pstats,
    summed, sstats, zrecv, zstats, result, table,
    in_sem, page_send, page_recv, own_sem, source_sem, q_send, q_recv,
    part_send, part_recv, pst_send, pst_recv, z_send, z_recv, zst_send, zst_recv,
    out_send, out_recv, fwd_send, fwd_recv,
):
    ctx, hd, pf = lax.axis_index("ctx"), lax.axis_index("hd"), lax.axis_index("pf")
    page_rows = pages.shape[0]
    rows = page_rows * REQS
    tokens = page_rows * PAGE
    device = (ctx * n_hd + hd) * n_pf + pf
    local_heads = KVH // n_hd
    per_req = local_heads * COLS
    own_reqs = REQS // n_pf
    plane_offsets = [(a, b) for a in range(n_hd) for b in range(n_pf) if a or b]

    def at(axis, index, offset, size):
        return {axis: lax.rem(index + offset, size)}

    barrier = pltpu.get_barrier_semaphore()
    for x in range(1, n_ctx):
        pl.semaphore_signal(barrier, inc=1, device_id_type=MESH, device_id={"ctx": ctx ^ x})
    for a, b in plane_offsets:
        pl.semaphore_signal(
            barrier, inc=1, device_id_type=MESH,
            device_id={**at("hd", hd, a, n_hd), **at("pf", pf, b, n_pf)},
        )
    greeted = n_ctx - 1 + len(plane_offsets)

    loads = [
        pltpu.make_async_copy(there, here, in_sem.at[index])
        for index, (there, here) in enumerate((
            (targets_h, targets), (pages_h, pages), (lengths_h, lengths), (freqs_h, freqs),
            (queries_h, queries), (counts_h, counts), (key_up_h, key_up),
            (value_up_h, value_up),
        ))
    ]
    for load in loads:
        load.start()
    loads[0].wait()

    total_pages = targets.shape[2]
    tall = jnp.concatenate([targets[r] for r in range(REQS)] * page_rows, axis=0)
    own_page = iota((rows, total_pages), 0) // REQS + device * page_rows
    target_col = jnp.sum(
        jnp.where(iota((rows, total_pages), 1) == own_page, tall, 0), axis=1, keepdims=True
    )
    down, across = iota((rows, rows), 0), iota((rows, rows), 1)
    target_row = jnp.sum(jnp.where(down == across, target_col, 0), axis=0, keepdims=True)
    earlier = jnp.where((target_row == target_col) & (across < down), 1, 0)
    slot_col = target_col * capacity + jnp.sum(earlier, axis=1, keepdims=True)
    width = source_v.shape[1]
    hit = slot_col == iota((rows, width), 1)
    source_v[...] = (
        jnp.sum(jnp.where(hit, iota((rows, width), 0) + 1, 0), axis=0, keepdims=True) - 1
    )
    to_scalars = pltpu.make_async_copy(source_v, source_s, source_sem)
    to_scalars.start()
    to_scalars.wait()
    loads[1].wait()

    def pack(block):
        def one(index, _):
            slot = block * capacity + index
            row = source_s[0, slot]
            safe = jnp.maximum(row, 0)
            page = pages[lax.div(safe, REQS), lax.rem(safe, REQS)]
            packed[slot] = jnp.where(row >= 0, page, jnp.zeros_like(page))
            return 0

        lax.fori_loop(0, capacity, one, 0, unroll=9)

    order = list(range(n_ctx // 2, n_ctx)) + list(range(1, n_ctx // 2))
    early, late, near = order[:n_ctx // 4], order[n_ctx // 4:n_ctx // 2], order[n_ctx // 2:]
    cuts = (EARLY * capacity // 36, LATE * capacity // 36, NEAR * capacity // 36)
    pieces = (
        [(x, 0, cuts[0]) for x in early] + [(x, 0, cuts[2]) for x in near],
        [(x, cuts[0], capacity) for x in early] + [(x, 0, cuts[1]) for x in late],
        [(x, cuts[1], capacity) for x in late] + [(x, cuts[2], capacity) for x in near],
    )
    page_copies = []

    def send_pages(stage):
        for x, low, high in pieces[stage]:
            if low == high:
                continue
            block = ctx ^ x
            slot = 2 * x + (1 if low else 0)
            copy = pltpu.make_async_remote_copy(
                src_ref=packed.at[pl.ds(block * capacity + low, high - low)],
                dst_ref=stored.at[pl.ds(ctx * capacity + low, high - low)],
                send_sem=page_send.at[slot],
                recv_sem=page_recv.at[slot],
                device_id={"ctx": block},
                device_id_type=MESH,
            )
            copy.start()
            page_copies.append(copy)

    for x in early + near:
        pack(ctx ^ x)
    pl.semaphore_wait(barrier, greeted)
    send_pages(0)
    for x in late:
        pack(ctx ^ x)
    pack(ctx)
    own_copy = pltpu.make_async_copy(
        packed.at[pl.ds(ctx * capacity, capacity)],
        stored.at[pl.ds(ctx * capacity, capacity)],
        own_sem,
    )
    own_copy.start()

    for load in loads[2:]:
        load.wait()
    lane = iota((REQS, HD_DIM), 1)
    sublane = iota((REQS, HD_DIM), 0)
    sign = jnp.where(lane < HD_DIM // 2, -1.0, 1.0).astype(jnp.float32)
    first_position = jnp.zeros((REQS, HD_DIM), jnp.int32)
    for r in range(REQS):
        first_position = jnp.where(sublane == r, lengths[r], first_position)
    frequency = jnp.broadcast_to(freqs[...], (REQS, HD_DIM))
    for s in range(STEPS):
        angle = (first_position + s).astype(jnp.float32) * frequency
        cosine, sine = jnp.cos(angle), jnp.sin(angle) * sign
        for head in range(local_heads * GROUP):
            k, g = head // GROUP, head % GROUP
            values = queries[s, :, head * HD_DIM:(head + 1) * HD_DIM].astype(jnp.float32)
            row = k * COLS + s * GROUP + g
            turned[row * REQS:(row + 1) * REQS, :] = (
                values * cosine + pltpu.roll(values, HD_DIM // 2, 1) * sine
            )
    for r in range(REQS):
        q_all[0, r] = turned[pl.ds(r, per_req, stride=REQS), :].astype(jnp.bfloat16)
    q_copies = []
    for a in range(1, n_hd):
        q_copies.append(
            pltpu.make_async_remote_copy(
                src_ref=q_all.at[0], dst_ref=q_all.at[a],
                send_sem=q_send.at[a], recv_sem=q_recv.at[a],
                device_id=at("hd", hd, a, n_hd), device_id_type=MESH,
            )
        )
        q_copies[-1].start()

    token = iota((tokens, HD_DIM), 0)
    angle = (device * tokens + token).astype(jnp.float32) * jnp.broadcast_to(
        freqs[...], (tokens, HD_DIM)
    )
    table[0] = jnp.cos(angle)
    table[1] = jnp.sin(angle) * jnp.where(iota((tokens, HD_DIM), 1) < HD_DIM // 2, -1.0, 1.0)

    pick = iota((total_pages, tokens), 0) == iota((total_pages, tokens), 1) // PAGE + device * page_rows
    spread_counts = jnp.dot(
        counts[...].astype(jnp.float32).astype(jnp.bfloat16),
        jnp.where(pick, 1.0, 0.0).astype(jnp.bfloat16),
        preferred_element_type=jnp.float32,
    )
    all_cols = KVH * COLS
    column = iota((all_cols, tokens), 1)
    step_of = iota((all_cols, tokens), 0) // GROUP % STEPS
    inside = (iota((1, tokens), 1) % PAGE).astype(jnp.float32)
    reach = device * tokens + column - step_of
    square = iota((LANES, LANES), 0) == iota((LANES, LANES), 1)
    request_of = iota((REQS, tokens), 0)

    for copy in q_copies:
        copy.wait()

    def part_copy(a, b, q):
        slot = a * n_pf + b
        other = lax.rem(pf + b, n_pf)
        return pltpu.make_async_remote_copy(
            src_ref=part.at[(n_hd - a) % n_hd, other * own_reqs + q],
            dst_ref=precv.at[slot, q],
            send_sem=part_send.at[slot, q], recv_sem=part_recv.at[slot, q],
            device_id={**at("hd", hd, a, n_hd), **at("pf", pf, b, n_pf)},
            device_id_type=MESH,
        )

    def attend(b, q):
        r = lax.rem(pf + b, n_pf) * own_reqs + q
        latent = pages[:, r].reshape(tokens, LATK + LATV)
        key_latent, value_latent = latent[:, :LATK], latent[:, LATK:]
        filled = jnp.sum(jnp.where(request_of == r, spread_counts, 0.0), axis=0, keepdims=True)
        valid = (inside < filled) & (reach <= lengths[r])
        scores = []
        for a in range(n_hd):
            owner = lax.rem(hd + n_hd - a, n_hd)
            start = pl.multiple_of(owner * local_heads * HD_DIM, HD_DIM)
            rebuilt = jnp.dot(
                key_latent, key_up[:, pl.ds(start, local_heads * HD_DIM)],
                preferred_element_type=jnp.float32,
            )
            for k in range(local_heads):
                plain = rebuilt[:, k * HD_DIM:(k + 1) * HD_DIM]
                keys = (
                    plain * table[0] + pltpu.roll(plain, HD_DIM // 2, 1) * table[1]
                ).astype(jnp.bfloat16)
                scores.append(lax.dot_general(
                    q_all[a, r, k * COLS:(k + 1) * COLS, :], keys,
                    (((1,), (1,)), ((), ())), preferred_element_type=jnp.float32,
                ))
        scores = jnp.concatenate(scores, axis=0) * (1.0 / math.sqrt(HD_DIM))
        masked = jnp.where(valid, scores, NEVER)
        peak = jnp.max(masked, axis=1, keepdims=True)
        weights = jnp.where(valid, jnp.exp(masked - peak), 0.0)
        total = jnp.sum(weights, axis=1, keepdims=True)
        numerator = jnp.dot(
            weights.astype(jnp.bfloat16), value_latent, preferred_element_type=jnp.float32
        ).astype(jnp.bfloat16)
        for a in range(n_hd):
            part[a, r] = numerator[a * per_req:(a + 1) * per_req]
            if a or b:
                part_copy((n_hd - a) % n_hd, b, q).start()
        for index, tall in enumerate((peak, total)):
            stats[index, pl.ds(r, 1), :] = jnp.sum(
                jnp.where(square, tall, 0.0), axis=0, keepdims=True
            )

    for b in list(range(1, n_pf)) + [0]:
        def one_request(q, _, b=b):
            attend(b, q)
            return 0

        lax.fori_loop(0, own_reqs, one_request, 0)

    plane = [
        pltpu.make_async_remote_copy(
            src_ref=stats, dst_ref=pstats.at[a * n_pf + b],
            send_sem=pst_send.at[a * n_pf + b], recv_sem=pst_recv.at[a * n_pf + b],
            device_id={**at("hd", hd, a, n_hd), **at("pf", pf, b, n_pf)},
            device_id_type=MESH,
        )
        for a, b in plane_offsets
    ]
    for copy in plane:
        copy.start()
    for copy in plane:
        copy.wait()

    def to_column(row, shift):
        there = iota((per_req, LANES), 1) == iota((per_req, LANES), 0) + shift
        return jnp.sum(
            jnp.where(there, jnp.broadcast_to(row, (per_req, LANES)), 0.0),
            axis=1, keepdims=True,
        )

    def merge(peaks, totals, numerators):
        top = functools.reduce(jnp.maximum, peaks)
        total = jnp.zeros_like(top)
        numerator = jnp.zeros(numerators[0].shape, jnp.float32)
        for peak, part_total, piece in zip(peaks, totals, numerators):
            factor = jnp.exp(peak - top)
            total = total + factor * part_total
            numerator = numerator + factor * piece.astype(jnp.float32)
        return top, total, numerator

    for q in range(own_reqs):
        request = pf * own_reqs + q
        for a, b in plane_offsets:
            part_copy(a, b, q).wait()
        peaks, totals, numerators = [], [], []
        for a, b in [(0, 0)] + plane_offsets:
            slot = a * n_pf + b
            shift = ((n_hd - a) % n_hd) * per_req
            if slot:
                pair = (pstats[slot, 0, pl.ds(request, 1), :], pstats[slot, 1, pl.ds(request, 1), :])
                numerators.append(precv[slot, q])
            else:
                pair = (stats[0, pl.ds(request, 1), :], stats[1, pl.ds(request, 1), :])
                numerators.append(part[0, request])
            peaks.append(to_column(pair[0], shift))
            totals.append(to_column(pair[1], shift))
        top, total, numerator = merge(peaks, totals, numerators)
        numerator = numerator.astype(jnp.bfloat16)
        for k in range(local_heads):
            summed[q, k * COLS:(k + 1) * COLS, :] = jnp.dot(
                numerator[k * COLS:(k + 1) * COLS],
                value_up[:, k * HD_DIM:(k + 1) * HD_DIM],
                preferred_element_type=jnp.float32,
            ).astype(jnp.bfloat16)
        corner = iota((per_req, LANES), 0) == iota((per_req, LANES), 1)
        for index, tall in enumerate((top, total)):
            sstats[index, q:q + 1, :] = jnp.sum(
                jnp.where(corner, tall, 0.0), axis=0, keepdims=True
            )

    def if_owner(index, body):
        if own_reqs >= n_ctx:
            body()
        else:
            pl.when(index < own_reqs)(body)

    def z_copies(x):
        other = ctx ^ x
        mine = other if own_reqs >= n_ctx else jnp.minimum(other, own_reqs - 1)
        return (
            pltpu.make_async_remote_copy(
                src_ref=summed.at[mine], dst_ref=zrecv.at[x],
                send_sem=z_send.at[x], recv_sem=z_recv.at[x],
                device_id={"ctx": other}, device_id_type=MESH,
            ),
            pltpu.make_async_remote_copy(
                src_ref=sstats, dst_ref=zstats.at[x],
                send_sem=zst_send.at[x], recv_sem=zst_recv.at[x],
                device_id={"ctx": other}, device_id_type=MESH,
            ),
        )

    def out_copy(x, came):
        owner = ctx ^ x if came else ctx
        return pltpu.make_async_remote_copy(
            src_ref=result.at[pf, owner], dst_ref=result.at[pf, owner],
            send_sem=out_send.at[x], recv_sem=out_recv.at[x],
            device_id={"ctx": ctx ^ x}, device_id_type=MESH,
        )

    def forward(x, b, came):
        place = lax.rem(pf + n_pf - b, n_pf) if came else pf
        slot = (b - 1) * n_ctx + x
        return pltpu.make_async_remote_copy(
            src_ref=result.at[place, ctx ^ x], dst_ref=result.at[place, ctx ^ x],
            send_sem=fwd_send.at[slot], recv_sem=fwd_recv.at[slot],
            device_id=at("pf", pf, b, n_pf), device_id_type=MESH,
        )

    for x in order:
        def start(x=x):
            for copy in z_copies(x):
                copy.start()
        if_owner(ctx ^ x, start)
    send_pages(1)

    def finish():
        for x in range(1, n_ctx):
            for copy in z_copies(x):
                copy.wait_recv()
        peaks = [to_column(sstats[0, pl.ds(ctx, 1), :], 0)]
        totals = [to_column(sstats[1, pl.ds(ctx, 1), :], 0)]
        numerators = [summed[ctx]]
        for x in range(1, n_ctx):
            peaks.append(to_column(zstats[x, 0, pl.ds(ctx, 1), :], 0))
            totals.append(to_column(zstats[x, 1, pl.ds(ctx, 1), :], 0))
            numerators.append(zrecv[x])
        top, total, numerator = merge(peaks, totals, numerators)
        result[pf, ctx] = (numerator / total).astype(jnp.bfloat16)
        for x in order:
            out_copy(x, False).start()
        for b in range(1, n_pf):
            forward(0, b, False).start()

    if_owner(ctx, finish)
    send_pages(2)
    for x in range(1, n_ctx):
        def passed_on(x=x):
            out_copy(x, True).wait_recv()
            for b in range(1, n_pf):
                forward(x, b, False).start()
        if_owner(ctx ^ x, passed_on)
    for x in range(n_ctx):
        def arrived(x=x):
            for b in range(1, n_pf):
                forward(x, b, True).wait_recv()
                forward(x, b, False).wait_send()
            if x:
                for copy in z_copies(x):
                    copy.wait_send()
        if_owner(ctx ^ x, arrived)

    def left():
        for x in range(1, n_ctx):
            out_copy(x, False).wait_send()

    if_owner(ctx, left)
    attended[...] = result[:, :own_reqs]
    own_copy.wait()
    for copy in page_copies:
        copy.wait()


def deliver(local_heads, stored_in, rows_in, stored, attended, rows, turned, pages, in_sem, out_sem, rows_sem):
    load = pltpu.make_async_copy(rows_in, rows, rows_sem)
    load.start()
    count = in_sem.shape[0]
    size = pages.shape[0] // count
    spans = [pl.ds(part * size, size) for part in range(count)]
    reads = [
        pltpu.make_async_copy(stored_in.at[span], pages.at[span], in_sem.at[part])
        for part, span in enumerate(spans)
    ]
    writes = [
        pltpu.make_async_copy(pages.at[span], stored.at[span], out_sem.at[part])
        for part, span in enumerate(spans)
    ]
    for copy in reads:
        copy.start()
    for read, write in zip(reads, writes):
        read.wait()
        write.start()
    load.wait()
    per_req = local_heads * COLS
    turned[...] = rows[...].reshape(turned.shape).astype(jnp.float32)
    for s in range(STEPS):
        for k in range(local_heads):
            for g in range(GROUP):
                row = k * COLS + s * GROUP + g
                column = (k * GROUP + g) * HD_DIM
                attended[s, :, column:column + HD_DIM] = turned[
                    pl.ds(row, REQS, stride=per_req), :
                ].astype(jnp.bfloat16)
    for copy in writes:
        copy.wait()


def on_device(latent_pages, page_target, page_count, context_length, queries, key_up, value_up):
    n_ctx, n_hd, n_pf = lax.axis_size("ctx"), lax.axis_size("hd"), lax.axis_size("pf")
    page_rows, request_count, page_length, latent_width = latent_pages.shape
    row_count = page_rows * request_count
    capacity = max(2, 9 * row_count // (8 * n_ctx))
    slot_count = n_ctx * capacity
    slot_lanes = -(-slot_count // LANES) * LANES
    local_heads = KVH // n_hd
    per_req = local_heads * COLS
    own_reqs = REQS // n_pf
    n_plane = n_hd * n_pf
    half = frequencies(HD_DIM)
    operands = (
        latent_pages, page_target.transpose(1, 2, 0), page_count.T, context_length,
        queries, key_up, value_up, jnp.asarray(np.concatenate([half, half])[None, :]),
    )
    hbm = pl.BlockSpec(memory_space=pltpu.HBM)
    bf16, f32 = jnp.bfloat16, jnp.float32
    vmem, dma = pltpu.VMEM, pltpu.SemaphoreType.DMA
    stored, rows = pl.pallas_call(
        functools.partial(kernel, n_ctx, n_hd, n_pf, capacity),
        out_shape=(
            jax.ShapeDtypeStruct((slot_count, page_length, latent_width), bf16),
            jax.ShapeDtypeStruct((n_pf, own_reqs, per_req, HD_DIM), bf16),
        ),
        in_specs=[hbm] * len(operands),
        out_specs=(pl.BlockSpec(memory_space=pl.ANY), pl.BlockSpec(memory_space=pltpu.VMEM)),
        scratch_shapes=[
            (pltpu.SMEM if index == 3 else vmem)(operand.shape, operand.dtype)
            for index, operand in enumerate(operands)
        ] + [
            vmem((slot_count, page_length, latent_width), bf16),
            vmem((1, slot_lanes), jnp.int32),
            pltpu.SMEM((1, slot_lanes), jnp.int32),
            vmem((per_req * REQS, HD_DIM), f32),
            vmem((n_hd, REQS, per_req, HD_DIM), bf16),
            vmem((n_hd, REQS, per_req, LATV), bf16),
            vmem((2, REQS, LANES), f32),
            vmem((n_plane, own_reqs, per_req, LATV), bf16),
            vmem((n_plane, 2, REQS, LANES), f32),
            vmem((own_reqs, per_req, HD_DIM), bf16),
            vmem((2, own_reqs, LANES), f32),
            vmem((n_ctx, per_req, HD_DIM), bf16),
            vmem((n_ctx, 2, own_reqs, LANES), f32),
            vmem((n_pf, n_ctx, per_req, HD_DIM), bf16),
            vmem((2, page_rows * PAGE, HD_DIM), f32),
            dma((len(operands),)),
            dma((2 * n_ctx,)), dma((2 * n_ctx,)), dma, dma, dma((n_hd,)), dma((n_hd,)),
            dma((n_plane, own_reqs)), dma((n_plane, own_reqs)), dma((n_plane,)), dma((n_plane,)),
            dma((n_ctx,)), dma((n_ctx,)), dma((n_ctx,)), dma((n_ctx,)),
            dma((n_ctx,)), dma((n_ctx,)), dma((n_ctx * n_pf,)), dma((n_ctx * n_pf,)),
        ],
        compiler_params=pltpu.CompilerParams(
            collective_id=0, has_side_effects=True, vmem_limit_bytes=58 * 1024 * 1024
        ),
    )(*operands)
    stored, attended = pl.pallas_call(
        functools.partial(deliver, local_heads),
        out_shape=(
            jax.ShapeDtypeStruct(stored.shape, bf16),
            jax.ShapeDtypeStruct(queries.shape, bf16),
        ),
        in_specs=[hbm, hbm],
        out_specs=(hbm, pl.BlockSpec(memory_space=pltpu.VMEM)),
        scratch_shapes=[
            vmem(rows.shape, bf16),
            vmem((REQS * per_req, HD_DIM), f32),
            vmem(stored.shape, bf16),
            dma((SPLITS,)),
            dma((SPLITS,)),
            dma,
        ],
        compiler_params=pltpu.CompilerParams(vmem_limit_bytes=58 * 1024 * 1024),
    )(stored, rows)
    return (attended, stored)


def solution(mesh):
    placed = (
        P(("ctx", "hd", "pf"), "grp", None, None),
        P(None, "grp", None),
        P(None, "grp"),
        P("grp"),
        P(None, "grp", "hd"),
        P(),
        P(None, "hd"),
    )
    return jax.shard_map(
        on_device,
        mesh=mesh,
        in_specs=placed,
        out_specs=(P(None, "grp", "hd"), P(("grp", "ctx", "hd", "pf"), None, None)),
        check_vma=False,
    )
```

```python
import functools
import math

import jax
import jax.numpy as jnp
import numpy as np
from jax import lax
from jax.experimental import pallas as pl
from jax.experimental.pallas import tpu as pltpu
from jax.sharding import PartitionSpec as P

KVH = 8
GROUP = 8
HD_DIM = 128
LATK = 256
LATV = 256
PAGE = 16
STEPS = 2
REQS = 8
COLS = STEPS * GROUP
LANES = 128
MESH = pl.DeviceIdType.MESH
NEVER = -1e30
SPLITS = 8
EARLY, LATE, NEAR = 36, 9, 36


def frequencies(head_width):
    exponent = np.arange(0, head_width, 2).astype(np.float32) / np.float32(head_width)
    inverse = np.power(np.float32(500000.0), -exponent).astype(np.float32)
    wavelength = np.float32(2.0 * math.pi) / inverse
    smooth = (np.float32(8192.0) / wavelength - np.float32(1.0)) / np.float32(3.0)
    mixed = (1.0 - smooth) * inverse / 8.0 + smooth * inverse
    return np.where(
        wavelength > 8192.0, inverse / 8.0, np.where(wavelength < 2048.0, inverse, mixed)
    ).astype(np.float32)


def iota(shape, dim):
    return lax.broadcasted_iota(jnp.int32, shape, dim)


def kernel(
    n_ctx, n_hd, n_pf, capacity,
    pages_h, targets_h, counts_h, lengths_h, queries_h, key_up_h, value_up_h, freqs_h,
    stored, attended,
    pages, targets, counts, lengths, queries, key_up, value_up, freqs,
    packed, source_v, source_s, turned, q_all, part, stats, precv, pstats,
    summed, sstats, zrecv, zstats, result, table,
    in_sem, page_send, page_recv, own_sem, source_sem, q_send, q_recv,
    part_send, part_recv, pst_send, pst_recv, z_send, z_recv, zst_send, zst_recv,
    out_send, out_recv, fwd_send, fwd_recv,
):
    ctx, hd, pf = lax.axis_index("ctx"), lax.axis_index("hd"), lax.axis_index("pf")
    page_rows = pages.shape[0]
    rows = page_rows * REQS
    tokens = page_rows * PAGE
    device = (ctx * n_hd + hd) * n_pf + pf
    local_heads = KVH // n_hd
    per_req = local_heads * COLS
    own_reqs = REQS // n_pf
    plane_offsets = [(a, b) for a in range(n_hd) for b in range(n_pf) if a or b]

    def at(axis, index, offset, size):
        return {axis: lax.rem(index + offset, size)}

    barrier = pltpu.get_barrier_semaphore()
    for x in range(1, n_ctx):
        pl.semaphore_signal(barrier, inc=1, device_id_type=MESH, device_id={"ctx": ctx ^ x})
    for a, b in plane_offsets:
        pl.semaphore_signal(
            barrier, inc=1, device_id_type=MESH,
            device_id={**at("hd", hd, a, n_hd), **at("pf", pf, b, n_pf)},
        )
    greeted = n_ctx - 1 + len(plane_offsets)

    loads = [
        pltpu.make_async_copy(there, here, in_sem.at[index])
        for index, (there, here) in enumerate((
            (targets_h, targets), (pages_h, pages), (lengths_h, lengths), (freqs_h, freqs),
            (queries_h, queries), (counts_h, counts), (key_up_h, key_up),
            (value_up_h, value_up),
        ))
    ]
    for load in loads:
        load.start()
    loads[0].wait()

    total_pages = targets.shape[2]
    tall = jnp.concatenate([targets[r] for r in range(REQS)] * page_rows, axis=0)
    own_page = iota((rows, total_pages), 0) // REQS + device * page_rows
    target_col = jnp.sum(
        jnp.where(iota((rows, total_pages), 1) == own_page, tall, 0), axis=1, keepdims=True
    )
    down, across = iota((rows, rows), 0), iota((rows, rows), 1)
    target_row = jnp.sum(jnp.where(down == across, target_col, 0), axis=0, keepdims=True)
    earlier = jnp.where((target_row == target_col) & (across < down), 1, 0)
    slot_col = target_col * capacity + jnp.sum(earlier, axis=1, keepdims=True)
    width = source_v.shape[1]
    hit = slot_col == iota((rows, width), 1)
    source_v[...] = (
        jnp.sum(jnp.where(hit, iota((rows, width), 0) + 1, 0), axis=0, keepdims=True) - 1
    )
    to_scalars = pltpu.make_async_copy(source_v, source_s, source_sem)
    to_scalars.start()
    to_scalars.wait()
    loads[1].wait()

    def pack(block):
        def one(index, _):
            slot = block * capacity + index
            row = source_s[0, slot]
            safe = jnp.maximum(row, 0)
            page = pages[lax.div(safe, REQS), lax.rem(safe, REQS)]
            packed[slot] = jnp.where(row >= 0, page, jnp.zeros_like(page))
            return 0

        lax.fori_loop(0, capacity, one, 0, unroll=9)

    order = list(range(n_ctx // 2, n_ctx)) + list(range(1, n_ctx // 2))
    early, late, near = order[:n_ctx // 4], order[n_ctx // 4:n_ctx // 2], order[n_ctx // 2:]
    cuts = (EARLY * capacity // 36, LATE * capacity // 36, NEAR * capacity // 36)
    pieces = (
        [(x, 0, cuts[0]) for x in early],
        [(x, 0, cuts[2]) for x in near],
        [(x, cuts[0], capacity) for x in early] + [(x, 0, cuts[1]) for x in late],
        [(x, cuts[1], capacity) for x in late] + [(x, cuts[2], capacity) for x in near],
    )
    page_copies = []

    def send_pages(stage):
        for x, low, high in pieces[stage]:
            if low == high:
                continue
            block = ctx ^ x
            slot = 2 * x + (1 if low else 0)
            copy = pltpu.make_async_remote_copy(
                src_ref=packed.at[pl.ds(block * capacity + low, high - low)],
                dst_ref=stored.at[pl.ds(ctx * capacity + low, high - low)],
                send_sem=page_send.at[slot],
                recv_sem=page_recv.at[slot],
                device_id={"ctx": block},
                device_id_type=MESH,
            )
            copy.start()
            page_copies.append(copy)

    for x in early:
        pack(ctx ^ x)
    pl.semaphore_wait(barrier, greeted)
    send_pages(0)
    for x in near:
        pack(ctx ^ x)
    send_pages(1)
    for x in late:
        pack(ctx ^ x)
    pack(ctx)
    own_copy = pltpu.make_async_copy(
        packed.at[pl.ds(ctx * capacity, capacity)],
        stored.at[pl.ds(ctx * capacity, capacity)],
        own_sem,
    )
    own_copy.start()

    for load in loads[2:]:
        load.wait()
    lane = iota((REQS, HD_DIM), 1)
    sublane = iota((REQS, HD_DIM), 0)
    sign = jnp.where(lane < HD_DIM // 2, -1.0, 1.0).astype(jnp.float32)
    first_position = jnp.zeros((REQS, HD_DIM), jnp.int32)
    for r in range(REQS):
        first_position = jnp.where(sublane == r, lengths[r], first_position)
    frequency = jnp.broadcast_to(freqs[...], (REQS, HD_DIM))
    for s in range(STEPS):
        angle = (first_position + s).astype(jnp.float32) * frequency
        cosine, sine = jnp.cos(angle), jnp.sin(angle) * sign
        for head in range(local_heads * GROUP):
            k, g = head // GROUP, head % GROUP
            values = queries[s, :, head * HD_DIM:(head + 1) * HD_DIM].astype(jnp.float32)
            row = k * COLS + s * GROUP + g
            turned[row * REQS:(row + 1) * REQS, :] = (
                values * cosine + pltpu.roll(values, HD_DIM // 2, 1) * sine
            )
    for r in range(REQS):
        q_all[0, r] = turned[pl.ds(r, per_req, stride=REQS), :].astype(jnp.bfloat16)
    q_copies = []
    for a in range(1, n_hd):
        q_copies.append(
            pltpu.make_async_remote_copy(
                src_ref=q_all.at[0], dst_ref=q_all.at[a],
                send_sem=q_send.at[a], recv_sem=q_recv.at[a],
                device_id=at("hd", hd, a, n_hd), device_id_type=MESH,
            )
        )
        q_copies[-1].start()

    token = iota((tokens, HD_DIM), 0)
    angle = (device * tokens + token).astype(jnp.float32) * jnp.broadcast_to(
        freqs[...], (tokens, HD_DIM)
    )
    table[0] = jnp.cos(angle)
    table[1] = jnp.sin(angle) * jnp.where(iota((tokens, HD_DIM), 1) < HD_DIM // 2, -1.0, 1.0)

    pick = iota((total_pages, tokens), 0) == iota((total_pages, tokens), 1) // PAGE + device * page_rows
    spread_counts = jnp.dot(
        counts[...].astype(jnp.float32).astype(jnp.bfloat16),
        jnp.where(pick, 1.0, 0.0).astype(jnp.bfloat16),
        preferred_element_type=jnp.float32,
    )
    all_cols = KVH * COLS
    column = iota((all_cols, tokens), 1)
    step_of = iota((all_cols, tokens), 0) // GROUP % STEPS
    inside = (iota((1, tokens), 1) % PAGE).astype(jnp.float32)
    reach = device * tokens + column - step_of
    square = iota((LANES, LANES), 0) == iota((LANES, LANES), 1)
    request_of = iota((REQS, tokens), 0)

    for copy in q_copies:
        copy.wait()

    def part_copy(a, b, q):
        slot = a * n_pf + b
        other = lax.rem(pf + b, n_pf)
        return pltpu.make_async_remote_copy(
            src_ref=part.at[(n_hd - a) % n_hd, other * own_reqs + q],
            dst_ref=precv.at[slot, q],
            send_sem=part_send.at[slot, q], recv_sem=part_recv.at[slot, q],
            device_id={**at("hd", hd, a, n_hd), **at("pf", pf, b, n_pf)},
            device_id_type=MESH,
        )

    def attend(b, q):
        r = lax.rem(pf + b, n_pf) * own_reqs + q
        latent = pages[:, r].reshape(tokens, LATK + LATV)
        key_latent, value_latent = latent[:, :LATK], latent[:, LATK:]
        filled = jnp.sum(jnp.where(request_of == r, spread_counts, 0.0), axis=0, keepdims=True)
        valid = (inside < filled) & (reach <= lengths[r])
        scores = []
        for a in range(n_hd):
            owner = lax.rem(hd + n_hd - a, n_hd)
            start = pl.multiple_of(owner * local_heads * HD_DIM, HD_DIM)
            rebuilt = jnp.dot(
                key_latent, key_up[:, pl.ds(start, local_heads * HD_DIM)],
                preferred_element_type=jnp.float32,
            )
            for k in range(local_heads):
                plain = rebuilt[:, k * HD_DIM:(k + 1) * HD_DIM]
                keys = (
                    plain * table[0] + pltpu.roll(plain, HD_DIM // 2, 1) * table[1]
                ).astype(jnp.bfloat16)
                scores.append(lax.dot_general(
                    q_all[a, r, k * COLS:(k + 1) * COLS, :], keys,
                    (((1,), (1,)), ((), ())), preferred_element_type=jnp.float32,
                ))
        scores = jnp.concatenate(scores, axis=0) * (1.0 / math.sqrt(HD_DIM))
        masked = jnp.where(valid, scores, NEVER)
        peak = jnp.max(masked, axis=1, keepdims=True)
        weights = jnp.where(valid, jnp.exp(masked - peak), 0.0)
        total = jnp.sum(weights, axis=1, keepdims=True)
        numerator = jnp.dot(
            weights.astype(jnp.bfloat16), value_latent, preferred_element_type=jnp.float32
        ).astype(jnp.bfloat16)
        for a in range(n_hd):
            part[a, r] = numerator[a * per_req:(a + 1) * per_req]
            if a or b:
                part_copy((n_hd - a) % n_hd, b, q).start()
        for index, tall in enumerate((peak, total)):
            stats[index, pl.ds(r, 1), :] = jnp.sum(
                jnp.where(square, tall, 0.0), axis=0, keepdims=True
            )

    for b in list(range(1, n_pf)) + [0]:
        def one_request(q, _, b=b):
            attend(b, q)
            return 0

        lax.fori_loop(0, own_reqs, one_request, 0)

    plane = [
        pltpu.make_async_remote_copy(
            src_ref=stats, dst_ref=pstats.at[a * n_pf + b],
            send_sem=pst_send.at[a * n_pf + b], recv_sem=pst_recv.at[a * n_pf + b],
            device_id={**at("hd", hd, a, n_hd), **at("pf", pf, b, n_pf)},
            device_id_type=MESH,
        )
        for a, b in plane_offsets
    ]
    for copy in plane:
        copy.start()
    for copy in plane:
        copy.wait()

    def to_column(row, shift):
        there = iota((per_req, LANES), 1) == iota((per_req, LANES), 0) + shift
        return jnp.sum(
            jnp.where(there, jnp.broadcast_to(row, (per_req, LANES)), 0.0),
            axis=1, keepdims=True,
        )

    def merge(peaks, totals, numerators):
        top = functools.reduce(jnp.maximum, peaks)
        total = jnp.zeros_like(top)
        numerator = jnp.zeros(numerators[0].shape, jnp.float32)
        for peak, part_total, piece in zip(peaks, totals, numerators):
            factor = jnp.exp(peak - top)
            total = total + factor * part_total
            numerator = numerator + factor * piece.astype(jnp.float32)
        return top, total, numerator

    for q in range(own_reqs):
        request = pf * own_reqs + q
        for a, b in plane_offsets:
            part_copy(a, b, q).wait()
        peaks, totals, numerators = [], [], []
        for a, b in [(0, 0)] + plane_offsets:
            slot = a * n_pf + b
            shift = ((n_hd - a) % n_hd) * per_req
            if slot:
                pair = (pstats[slot, 0, pl.ds(request, 1), :], pstats[slot, 1, pl.ds(request, 1), :])
                numerators.append(precv[slot, q])
            else:
                pair = (stats[0, pl.ds(request, 1), :], stats[1, pl.ds(request, 1), :])
                numerators.append(part[0, request])
            peaks.append(to_column(pair[0], shift))
            totals.append(to_column(pair[1], shift))
        top, total, numerator = merge(peaks, totals, numerators)
        numerator = numerator.astype(jnp.bfloat16)
        for k in range(local_heads):
            summed[q, k * COLS:(k + 1) * COLS, :] = jnp.dot(
                numerator[k * COLS:(k + 1) * COLS],
                value_up[:, k * HD_DIM:(k + 1) * HD_DIM],
                preferred_element_type=jnp.float32,
            ).astype(jnp.bfloat16)
        corner = iota((per_req, LANES), 0) == iota((per_req, LANES), 1)
        for index, tall in enumerate((top, total)):
            sstats[index, q:q + 1, :] = jnp.sum(
                jnp.where(corner, tall, 0.0), axis=0, keepdims=True
            )

    def if_owner(index, body):
        if own_reqs >= n_ctx:
            body()
        else:
            pl.when(index < own_reqs)(body)

    def z_copies(x):
        other = ctx ^ x
        mine = other if own_reqs >= n_ctx else jnp.minimum(other, own_reqs - 1)
        return (
            pltpu.make_async_remote_copy(
                src_ref=summed.at[mine], dst_ref=zrecv.at[x],
                send_sem=z_send.at[x], recv_sem=z_recv.at[x],
                device_id={"ctx": other}, device_id_type=MESH,
            ),
            pltpu.make_async_remote_copy(
                src_ref=sstats, dst_ref=zstats.at[x],
                send_sem=zst_send.at[x], recv_sem=zst_recv.at[x],
                device_id={"ctx": other}, device_id_type=MESH,
            ),
        )

    def out_copy(x, came):
        owner = ctx ^ x if came else ctx
        return pltpu.make_async_remote_copy(
            src_ref=result.at[pf, owner], dst_ref=result.at[pf, owner],
            send_sem=out_send.at[x], recv_sem=out_recv.at[x],
            device_id={"ctx": ctx ^ x}, device_id_type=MESH,
        )

    def forward(x, b, came):
        place = lax.rem(pf + n_pf - b, n_pf) if came else pf
        slot = (b - 1) * n_ctx + x
        return pltpu.make_async_remote_copy(
            src_ref=result.at[place, ctx ^ x], dst_ref=result.at[place, ctx ^ x],
            send_sem=fwd_send.at[slot], recv_sem=fwd_recv.at[slot],
            device_id=at("pf", pf, b, n_pf), device_id_type=MESH,
        )

    for x in order:
        def start(x=x):
            for copy in z_copies(x):
                copy.start()
        if_owner(ctx ^ x, start)
    send_pages(2)

    def finish():
        for x in range(1, n_ctx):
            for copy in z_copies(x):
                copy.wait_recv()
        peaks = [to_column(sstats[0, pl.ds(ctx, 1), :], 0)]
        totals = [to_column(sstats[1, pl.ds(ctx, 1), :], 0)]
        numerators = [summed[ctx]]
        for x in range(1, n_ctx):
            peaks.append(to_column(zstats[x, 0, pl.ds(ctx, 1), :], 0))
            totals.append(to_column(zstats[x, 1, pl.ds(ctx, 1), :], 0))
            numerators.append(zrecv[x])
        top, total, numerator = merge(peaks, totals, numerators)
        result[pf, ctx] = (numerator / total).astype(jnp.bfloat16)
        for x in order:
            out_copy(x, False).start()
        for b in range(1, n_pf):
            forward(0, b, False).start()

    if_owner(ctx, finish)
    send_pages(3)
    for x in range(1, n_ctx):
        def passed_on(x=x):
            out_copy(x, True).wait_recv()
            for b in range(1, n_pf):
                forward(x, b, False).start()
        if_owner(ctx ^ x, passed_on)
    for x in range(n_ctx):
        def arrived(x=x):
            for b in range(1, n_pf):
                forward(x, b, True).wait_recv()
                forward(x, b, False).wait_send()
            if x:
                for copy in z_copies(x):
                    copy.wait_send()
        if_owner(ctx ^ x, arrived)

    def left():
        for x in range(1, n_ctx):
            out_copy(x, False).wait_send()

    if_owner(ctx, left)
    attended[...] = result[:, :own_reqs]
    own_copy.wait()
    for copy in page_copies:
        copy.wait()


def deliver(local_heads, stored_in, rows_in, stored, attended, rows, turned, pages, in_sem, out_sem, rows_sem):
    load = pltpu.make_async_copy(rows_in, rows, rows_sem)
    load.start()
    count = in_sem.shape[0]
    size = pages.shape[0] // count
    spans = [pl.ds(part * size, size) for part in range(count)]
    reads = [
        pltpu.make_async_copy(stored_in.at[span], pages.at[span], in_sem.at[part])
        for part, span in enumerate(spans)
    ]
    writes = [
        pltpu.make_async_copy(pages.at[span], stored.at[span], out_sem.at[part])
        for part, span in enumerate(spans)
    ]
    for copy in reads:
        copy.start()
    for read, write in zip(reads, writes):
        read.wait()
        write.start()
    load.wait()
    per_req = local_heads * COLS
    turned[...] = rows[...].reshape(turned.shape).astype(jnp.float32)
    for s in range(STEPS):
        for k in range(local_heads):
            for g in range(GROUP):
                row = k * COLS + s * GROUP + g
                column = (k * GROUP + g) * HD_DIM
                attended[s, :, column:column + HD_DIM] = turned[
                    pl.ds(row, REQS, stride=per_req), :
                ].astype(jnp.bfloat16)
    for copy in writes:
        copy.wait()


def on_device(latent_pages, page_target, page_count, context_length, queries, key_up, value_up):
    n_ctx, n_hd, n_pf = lax.axis_size("ctx"), lax.axis_size("hd"), lax.axis_size("pf")
    page_rows, request_count, page_length, latent_width = latent_pages.shape
    row_count = page_rows * request_count
    capacity = max(2, 9 * row_count // (8 * n_ctx))
    slot_count = n_ctx * capacity
    slot_lanes = -(-slot_count // LANES) * LANES
    local_heads = KVH // n_hd
    per_req = local_heads * COLS
    own_reqs = REQS // n_pf
    n_plane = n_hd * n_pf
    half = frequencies(HD_DIM)
    operands = (
        latent_pages, page_target.transpose(1, 2, 0), page_count.T, context_length,
        queries, key_up, value_up, jnp.asarray(np.concatenate([half, half])[None, :]),
    )
    hbm = pl.BlockSpec(memory_space=pltpu.HBM)
    bf16, f32 = jnp.bfloat16, jnp.float32
    vmem, dma = pltpu.VMEM, pltpu.SemaphoreType.DMA
    stored, rows = pl.pallas_call(
        functools.partial(kernel, n_ctx, n_hd, n_pf, capacity),
        out_shape=(
            jax.ShapeDtypeStruct((slot_count, page_length, latent_width), bf16),
            jax.ShapeDtypeStruct((n_pf, own_reqs, per_req, HD_DIM), bf16),
        ),
        in_specs=[hbm] * len(operands),
        out_specs=(pl.BlockSpec(memory_space=pl.ANY), pl.BlockSpec(memory_space=pltpu.VMEM)),
        scratch_shapes=[
            (pltpu.SMEM if index == 3 else vmem)(operand.shape, operand.dtype)
            for index, operand in enumerate(operands)
        ] + [
            vmem((slot_count, page_length, latent_width), bf16),
            vmem((1, slot_lanes), jnp.int32),
            pltpu.SMEM((1, slot_lanes), jnp.int32),
            vmem((per_req * REQS, HD_DIM), f32),
            vmem((n_hd, REQS, per_req, HD_DIM), bf16),
            vmem((n_hd, REQS, per_req, LATV), bf16),
            vmem((2, REQS, LANES), f32),
            vmem((n_plane, own_reqs, per_req, LATV), bf16),
            vmem((n_plane, 2, REQS, LANES), f32),
            vmem((own_reqs, per_req, HD_DIM), bf16),
            vmem((2, own_reqs, LANES), f32),
            vmem((n_ctx, per_req, HD_DIM), bf16),
            vmem((n_ctx, 2, own_reqs, LANES), f32),
            vmem((n_pf, n_ctx, per_req, HD_DIM), bf16),
            vmem((2, page_rows * PAGE, HD_DIM), f32),
            dma((len(operands),)),
            dma((2 * n_ctx,)), dma((2 * n_ctx,)), dma, dma, dma((n_hd,)), dma((n_hd,)),
            dma((n_plane, own_reqs)), dma((n_plane, own_reqs)), dma((n_plane,)), dma((n_plane,)),
            dma((n_ctx,)), dma((n_ctx,)), dma((n_ctx,)), dma((n_ctx,)),
            dma((n_ctx,)), dma((n_ctx,)), dma((n_ctx * n_pf,)), dma((n_ctx * n_pf,)),
        ],
        compiler_params=pltpu.CompilerParams(
            collective_id=0, has_side_effects=True, vmem_limit_bytes=58 * 1024 * 1024
        ),
    )(*operands)
    stored, attended = pl.pallas_call(
        functools.partial(deliver, local_heads),
        out_shape=(
            jax.ShapeDtypeStruct(stored.shape, bf16),
            jax.ShapeDtypeStruct(queries.shape, bf16),
        ),
        in_specs=[hbm, hbm],
        out_specs=(hbm, pl.BlockSpec(memory_space=pltpu.VMEM)),
        scratch_shapes=[
            vmem(rows.shape, bf16),
            vmem((REQS * per_req, HD_DIM), f32),
            vmem(stored.shape, bf16),
            dma((SPLITS,)),
            dma((SPLITS,)),
            dma,
        ],
        compiler_params=pltpu.CompilerParams(vmem_limit_bytes=58 * 1024 * 1024),
    )(stored, rows)
    return (attended, stored)


def solution(mesh):
    placed = (
        P(("ctx", "hd", "pf"), "grp", None, None),
        P(None, "grp", None),
        P(None, "grp"),
        P("grp"),
        P(None, "grp", "hd"),
        P(),
        P(None, "hd"),
    )
    return jax.shard_map(
        on_device,
        mesh=mesh,
        in_specs=placed,
        out_specs=(P(None, "grp", "hd"), P(("grp", "ctx", "hd", "pf"), None, None)),
        check_vma=False,
    )
```
